32 devices in a mesh: row: 4 (over z), col: 4 (over x, core), layer: 2 (over y).
Axes of the slice: x: 2, y: 2, z: 4, core: 2. Of those that a mesh axis runs over, the one named last changes fastest.
Arguments:
- density: float32 [2, 2048, 1024], P('layer', 'row', 'col'), may hold values from -6 to 6
- dens_mask: int32 [2, 32, 16], P('layer', 'row', 'col'), may hold values from 0 to 1, as said below
- hamiltonian: float32 [2, 1024, 8192], P('layer', 'row', 'col'), may hold values from -0.375 to 0.375
- ham_mask: int32 [2, 16, 128], P('layer', None, 'col'), may hold values from 0 to 1, as said below
- filter_mask: int32 [32, 128], P('row', 'col'), may hold values from 0 to 1, as said below
Outputs:
- product: float32 [2048, 8192], P('row', ('col', 'layer'))
The draws below stay inside these ranges and needn't reach their ends.
Inputs may be any that keep to these rules, and one draw needn't show every extreme that they name: `dens_mask`: 1 where a density block is nonzero, else 0. `ham_mask`: 1 where a Hamiltonian block is nonzero, else 0. `filter_mask`: 1 where a result block is kept, else 0.
All inputs are finite; a program needn't handle non-finite values.
Results may differ from the reference program's by a relative error of at most 0.0001.
Values sent between devices are 32-bit elements; how exact they have to be, the bound alone decides.
A program may use at most 128 MiB of HBM per device.

```python
import jax
import jax.numpy as jnp
from jax import lax

BLOCK = 64
MB_ALL = 32
KB_HALF = 16
NB_ALL = 128
N_LAYER = 2


def band_mask(key, row_pos, col_pos):
    key_shift, key_width, key_extra = jax.random.split(key, 3)
    offset = jax.random.randint(key_shift, (), 0, 1000, dtype=jnp.int32)
    widths = jax.random.randint(key_width, row_pos.shape, 150, 450, dtype=jnp.int32)
    apart = jnp.abs(row_pos[:, None] - (col_pos[None, :] + offset) % 1000)
    cyclic = jnp.minimum(apart, 1000 - apart)
    scatter = jax.random.randint(key_extra, cyclic.shape, 0, 100, dtype=jnp.int32) < 10
    return ((cyclic < widths[:, None]) | scatter).astype(jnp.int32)


def draw_dens_mask(key, part):
    inner_total = N_LAYER * KB_HALF
    row_pos = jnp.arange(MB_ALL, dtype=jnp.int32) * 1000 // MB_ALL
    inner_pos = jnp.arange(inner_total, dtype=jnp.int32) * 1000 // inner_total
    whole = band_mask(jax.random.fold_in(key, 11), row_pos, inner_pos)
    return jnp.transpose(whole.reshape(MB_ALL, N_LAYER, KB_HALF), (1, 0, 2))


def draw_ham_mask(key, part):
    inner_total = N_LAYER * KB_HALF
    inner_pos = jnp.arange(inner_total, dtype=jnp.int32) * 1000 // inner_total
    col_pos = jnp.arange(NB_ALL, dtype=jnp.int32) * 1000 // NB_ALL
    whole = band_mask(jax.random.fold_in(key, 23), inner_pos, col_pos)
    return whole.reshape(N_LAYER, KB_HALF, NB_ALL)


def draw_filter_mask(key, part):
    row_pos = jnp.arange(MB_ALL, dtype=jnp.int32) * 1000 // MB_ALL
    col_pos = jnp.arange(NB_ALL, dtype=jnp.int32) * 1000 // NB_ALL
    return band_mask(jax.random.fold_in(key, 37), row_pos, col_pos)


def steps_of(rng, extent, pieces, least, top_value):
    def one(dim, blocks):
        steps = jax.random.uniform(jax.random.fold_in(jax.random.fold_in(rng, 6), dim), (blocks,), jnp.float32, least / len(pieces), top_value / len(pieces))
        return jnp.repeat(jnp.exp(steps), extent[dim] // blocks).reshape((-1,) + (1,) * (len(extent) - dim - 1))

    loudness = one(*pieces[0])
    for cut in pieces[1:]:
        loudness = loudness * one(*cut)
    return loudness


def scatter_about(stream_key, dims, scale, most, cuts=(), held_as=jnp.bfloat16):
    entries = jax.random.normal(stream_key, dims, jnp.float32) * scale
    if len(cuts) > 0:
        entries = steps_of(stream_key, dims, cuts, -0.22, 0.18) * entries
    return jnp.clip(entries, min=-most, max=most).astype(held_as)


def setup_inputs(seed: int = 0) -> dict:
    key_list = jax.random.split(jax.random.key(seed), 6)
    return {
        "density": scatter_about(key_list[0], (N_LAYER, MB_ALL * BLOCK, KB_HALF * BLOCK), 1.0, 6.0, ((0, 2), (1, 4), (2, 4)), jnp.float32),
        "dens_mask": draw_dens_mask(jax.random.fold_in(key_list[5], 71), 0),
        "hamiltonian": scatter_about(key_list[2], (N_LAYER, KB_HALF * BLOCK, NB_ALL * BLOCK), (BLOCK * 4) ** -0.5, 0.375, ((0, 2), (1, 4), (2, 4)), jnp.float32),
        "ham_mask": draw_ham_mask(jax.random.fold_in(key_list[5], 71), 0),
        "filter_mask": draw_filter_mask(jax.random.fold_in(key_list[5], 71), 0),
    }


def expand(block_mask):
    widened = jnp.repeat(block_mask.astype(jnp.float32), BLOCK, axis=-2)
    return jnp.repeat(widened, BLOCK, axis=-1)


def reference(density, dens_mask, hamiltonian, ham_mask, filter_mask):
    dens_eff = density * expand(dens_mask)
    ham_eff = hamiltonian * expand(ham_mask)
    total = jnp.dot(dens_eff[0], ham_eff[0], precision=lax.Precision.HIGHEST, preferred_element_type=jnp.float32)
    for group_pos in range(1, N_LAYER):
        total = total + jnp.dot(dens_eff[group_pos], ham_eff[group_pos], precision=lax.Precision.HIGHEST, preferred_element_type=jnp.float32)
    return total * expand(filter_mask)
```

```python
import functools

import jax
import jax.numpy as jnp
from jax import lax
from jax.experimental import pallas as pl
from jax.experimental.pallas import tpu as pltpu
from jax.sharding import PartitionSpec as P

BLOCK = 64
CHUNKS = 4


def expand(block_mask):
    widened = jnp.repeat(block_mask.astype(jnp.float32), BLOCK, axis=-2)
    return jnp.repeat(widened, BLOCK, axis=-1)


def masked_ham(hamiltonian, ham_mask):
    blocks = hamiltonian.shape[1] // BLOCK
    mine = lax.dynamic_slice_in_dim(ham_mask[0], lax.axis_index("row") * blocks, blocks, 0)
    wide = jnp.repeat(mine.astype(jnp.float32), BLOCK, axis=1)
    ham = hamiltonian[0].reshape(blocks, BLOCK, -1) * wide[:, None, :]
    return ham.reshape(hamiltonian.shape[1:])


def split(x):
    high = x.astype(jnp.bfloat16)
    return high, (x - high.astype(jnp.float32)).astype(jnp.bfloat16)


def kernel(
    d_ref, h_ref, out_ref,
    dbuf, hbuf, dhi, dlo, hhi, hlo, mine, ends,
    d_sem, h_sem, res_sem, send_sem, res_send, local_sem, y_sem,
):
    r, c, l = lax.axis_index("row"), lax.axis_index("col"), lax.axis_index("layer")
    rows, width = d_ref.shape
    depth = h_ref.shape[0]
    cols = out_ref.shape[1]
    cw = cols // CHUNKS
    across = (c + 2) % 4
    sibling = c + 1 - 2 * (c % 2)
    other = 1 - l
    is_hub = jnp.logical_and(r > 0, r < 3)

    def at(row, col, layer):
        return {"row": row, "col": col, "layer": layer}

    def send(src, dst, sem, recv, where):
        copy = pltpu.make_async_remote_copy(
            src_ref=src, dst_ref=dst, send_sem=sem, recv_sem=recv,
            device_id=where, device_id_type=pl.DeviceIdType.MESH,
        )
        copy.start()
        return copy

    def arrived(ref, recv):
        pltpu.make_async_remote_copy(
            src_ref=ref, dst_ref=ref, send_sem=send_sem.at[0], recv_sem=recv,
            device_id=at(r, c, other), device_id_type=pl.DeviceIdType.MESH,
        ).wait_recv()

    def ham_rows(row, layer):
        return pl.ds(pl.multiple_of((row * 2 + layer) * depth, depth), depth)

    def chunk(j):
        return pl.ds(pl.multiple_of(j * cw, cw), cw)

    def piece(slot, half):
        return dbuf.at[slot, pl.ds(half * rows, rows), :]

    def ham_from(layer, j):
        return h_ref.at[:, pl.ds(pl.multiple_of(layer * cols + j * cw, cw), cw)]

    barrier = pltpu.get_barrier_semaphore()

    def greet(partners):
        for where in partners:
            pl.semaphore_signal(barrier, inc=1, device_id=where, device_id_type=pl.DeviceIdType.MESH)
        pl.semaphore_wait(barrier, len(partners))

    @pl.when(jnp.logical_not(is_hub))
    def _():
        hub = 1 + r // 3
        greet([at(hub, c, l), at(hub, c, other)])
        first = send(d_ref, piece(c * 2 + l, 1), send_sem.at[0], d_sem.at[c * 2 + l, 1], at(hub, c, l))
        first.wait_send()
        sent = []
        for j in range(CHUNKS):
            for layer, k in ((l, 0), (other, 1)):
                sent.append(send(
                    ham_from(layer, j), hbuf.at[ham_rows(r, l), chunk(j)],
                    send_sem.at[1 + 2 * j + k], h_sem.at[r, l, j], at(hub, c, layer),
                ))
        kept = []
        for j in range(CHUNKS):
            arrived(ends.at[:, chunk(j)], res_sem.at[j])
            keep = pltpu.make_async_copy(ends.at[:, chunk(j)], out_ref.at[:, chunk(j)], local_sem.at[j])
            keep.start()
            kept.append(keep)
        for copy in sent:
            copy.wait_send()
        for copy in kept:
            copy.wait()

    @pl.when(is_hub)
    def _():
        far, end = 3 - r, 3 * r - 3
        far_end = 3 - end
        greet([
            at(r, c, other), at(r, across, l), at(r, sibling, l),
            at(end, c, l), at(end, c, other), at(far, c, l), at(far, c, other),
        ])
        own = c * 2 + l
        sent = []

        def push(src, dst, recv, where):
            sent.append(send(src, dst, send_sem.at[len(sent)], recv, where))

        def absorb(slot, half):
            def tile(i, _):
                at_rows = pl.ds(pl.multiple_of(half * rows + i * 128, 128), 128)
                high, low = split(dbuf[slot, at_rows, :])
                at_cols = pl.ds(pl.multiple_of(slot * width, width), width)
                dhi[at_rows, at_cols] = high
                dlo[at_rows, at_cols] = low
                return 0

            lax.fori_loop(0, rows // 128, tile, 0)

        def pass_on(src, slot, half, partners):
            for where in partners:
                push(src, piece(slot, half), d_sem.at[slot, half], where)

        y, x, s = at(r, c, other), at(r, across, l), at(r, sibling, l)

        local_d = pltpu.make_async_copy(d_ref, piece(own, 0), local_sem.at[0])
        local_d.start()
        local_h = pltpu.make_async_copy(
            h_ref.at[:, pl.ds(pl.multiple_of(l * cols, cols), cols)],
            hbuf.at[ham_rows(r, l), :], local_sem.at[1],
        )
        local_h.start()
        pass_on(d_ref, own, 0, (y, x, s))
        for j in range(CHUNKS):
            for layer in (l, other):
                push(
                    ham_from(layer, j), hbuf.at[ham_rows(r, l), chunk(j)],
                    h_sem.at[r, l, j], at(far, c, layer),
                )
        local_d.wait()
        absorb(own, 0)

        def take(slot, half, partners):
            arrived(piece(slot, half), d_sem.at[slot, half])
            pass_on(piece(slot, half), slot, half, partners)
            absorb(slot, half)

        take(own, 1, (y, x, s))
        push(
            h_ref.at[:, pl.ds(pl.multiple_of(other * cols, cols), cols)],
            hbuf.at[ham_rows(r, l), :], y_sem, y,
        )
        take(c * 2 + other, 0, (x, s))

        def relay(j):
            for layer in range(2):
                ref = hbuf.at[ham_rows(end, layer), chunk(j)]
                arrived(ref, h_sem.at[end, layer, j])
                push(ref, ref, h_sem.at[end, layer, j], at(far, c, l))

        relay(0)
        take(c * 2 + other, 1, (x, s))
        take(across * 2 + l, 0, (s,))
        for j in range(1, CHUNKS // 2):
            relay(j)
        take(across * 2 + l, 1, (s,))
        take(across * 2 + other, 0, (s,))
        for j in range(CHUNKS // 2, CHUNKS):
            relay(j)
        take(across * 2 + other, 1, (s,))
        far_sibling = (sibling + 2) % 4
        for col in (sibling, far_sibling):
            for layer in (l, other):
                for half in range(2):
                    take(col * 2 + layer, half, ())
        local_h.wait()
        arrived(hbuf.at[ham_rows(r, other), :], y_sem)

        def rows_of(first, target, j):
            def tile(i, _):
                at_rows = pl.ds(pl.multiple_of(first + i * 256, 256), 256)
                high = dhi[at_rows, :]
                total = jnp.dot(high, hhi[...], preferred_element_type=jnp.float32)
                total += jnp.dot(high, hlo[...], preferred_element_type=jnp.float32)
                total += jnp.dot(dlo[at_rows, :], hhi[...], preferred_element_type=jnp.float32)
                target[pl.ds(pl.multiple_of(i * 256, 256), 256), chunk(j)] = total
                return 0

            lax.fori_loop(0, rows // 256, tile, 0)

        def result(j):
            return pltpu.make_async_remote_copy(
                src_ref=ends.at[:, chunk(j)], dst_ref=ends.at[:, chunk(j)],
                send_sem=res_send.at[j], recv_sem=res_sem.at[j],
                device_id=at(end, c, l), device_id_type=pl.DeviceIdType.MESH,
            )

        def keep(j):
            return pltpu.make_async_copy(mine.at[:, chunk(j)], out_ref.at[:, chunk(j)], local_sem.at[2 + j])

        def step(j, _):
            for row in (far, far_end):
                for layer in range(2):
                    arrived(hbuf.at[ham_rows(row, layer), chunk(j)], h_sem.at[row, layer, j])

            def part(i, _):
                at_rows = pl.ds(pl.multiple_of(i * 256, 256), 256)
                high, low = split(hbuf[at_rows, chunk(j)])
                hhi[at_rows, :] = high
                hlo[at_rows, :] = low
                return 0

            lax.fori_loop(0, hbuf.shape[0] // 256, part, 0)
            rows_of(rows, ends, j)
            result(j).start()
            rows_of(0, mine, j)
            keep(j).start()
            return 0

        lax.fori_loop(0, CHUNKS, step, 0)
        for copy in sent:
            copy.wait_send()
        for j in range(CHUNKS):
            result(j).wait_send()
            keep(j).wait()


def product_of(dens, ham, layers, grid_cols):
    rows, width = dens.shape
    depth, ham_cols = ham.shape
    cols = ham_cols // layers
    inner = layers * grid_cols * width
    f32, bf16 = jnp.float32, jnp.bfloat16
    dma = pltpu.SemaphoreType.DMA
    return pl.pallas_call(
        kernel,
        out_shape=jax.ShapeDtypeStruct((rows, cols), f32),
        in_specs=[pl.BlockSpec(memory_space=pl.ANY)] * 2,
        out_specs=pl.BlockSpec(memory_space=pl.ANY),
        scratch_shapes=[
            pltpu.VMEM((layers * grid_cols, 2 * rows, width), f32),
            pltpu.VMEM((inner, cols), f32),
            pltpu.VMEM((2 * rows, inner), bf16),
            pltpu.VMEM((2 * rows, inner), bf16),
            pltpu.VMEM((inner, cols // CHUNKS), bf16),
            pltpu.VMEM((inner, cols // CHUNKS), bf16),
            pltpu.VMEM((rows, cols), f32),
            pltpu.VMEM((rows, cols), f32),
            dma((layers * grid_cols, 2)),
            dma((4, 2, CHUNKS)),
            dma((CHUNKS,)),
            dma((16 + 4 * CHUNKS,)),
            dma((CHUNKS,)),
            dma((2 + CHUNKS,)),
            dma,
        ],
        compiler_params=pltpu.CompilerParams(
            collective_id=0, has_side_effects=True, vmem_limit_bytes=48 * 2**20
        ),
    )(dens, ham)


def lined_up(density, dens_mask, hamiltonian, ham_mask, filter_mask, *, layers, grid_cols):
    dens = density[0] * expand(dens_mask[0])
    ham = masked_ham(hamiltonian, ham_mask)
    total = product_of(dens, ham, layers, grid_cols)
    kept_blocks = filter_mask.shape[1] // layers
    kept = lax.dynamic_slice_in_dim(filter_mask, lax.axis_index("layer") * kept_blocks, kept_blocks, 1)
    wide = jnp.repeat(kept.astype(jnp.float32), BLOCK, axis=1)
    out = total.reshape(-1, BLOCK, total.shape[1]) * wide[:, None, :]
    return out.reshape(total.shape)


def gathered(density, dens_mask, hamiltonian, ham_mask, filter_mask):
    dens = lax.all_gather(density * expand(dens_mask), "col", axis=2, tiled=True)[0]
    ham = lax.all_gather(masked_ham(hamiltonian, ham_mask), "row", axis=0, tiled=True)
    part = jnp.dot(dens, ham, precision=lax.Precision.HIGHEST, preferred_element_type=jnp.float32)
    return lax.psum_scatter(part * expand(filter_mask), "layer", scatter_dimension=1, tiled=True)


def solution(mesh):
    sizes = dict(mesh.shape)
    layers, grid_cols = sizes["layer"], sizes["col"]
    body = gathered
    if sizes == {"row": 4, "col": 4, "layer": 2}:
        body = functools.partial(lined_up, layers=layers, grid_cols=grid_cols)
    return jax.shard_map(
        body,
        mesh=mesh,
        in_specs=(
            P("layer", "row", "col"),
            P("layer", "row", "col"),
            P("layer", "row", "col"),
            P("layer", None, "col"),
            P("row", "col"),
        ),
        out_specs=P("row", ("col", "layer")),
        check_vma=False,
    )
```

```python
import functools

import jax
import jax.numpy as jnp
from jax import lax
from jax.experimental import pallas as pl
from jax.experimental.pallas import tpu as pltpu
from jax.sharding import PartitionSpec as P

BLOCK = 64


def expand(block_mask):
    widened = jnp.repeat(block_mask.astype(jnp.float32), BLOCK, axis=-2)
    return jnp.repeat(widened, BLOCK, axis=-1)


def masked_ham(hamiltonian, ham_mask):
    blocks = hamiltonian.shape[1] // BLOCK
    mine = lax.dynamic_slice_in_dim(ham_mask[0], lax.axis_index("row") * blocks, blocks, 0)
    wide = jnp.repeat(mine.astype(jnp.float32), BLOCK, axis=1)
    ham = hamiltonian[0].reshape(blocks, BLOCK, -1) * wide[:, None, :]
    return ham.reshape(hamiltonian.shape[1:])


def split(x):
    high = x.astype(jnp.bfloat16)
    return high, (x - high.astype(jnp.float32)).astype(jnp.bfloat16)


def kernel(
    d_ref, h_ref, out_ref,
    dbuf, hbuf, dhi, dlo, hhi, hlo, mine, ends,
    d_sem, h_sem, res_sem, send_sem, res_send, local_sem,
):
    r, c, l = lax.axis_index("row"), lax.axis_index("col"), lax.axis_index("layer")
    rows, width = d_ref.shape
    depth = h_ref.shape[0]
    cols = out_ref.shape[1]
    spans = chunk_spans(cols)
    across = (c + 2) % 4
    sibling = c + 1 - 2 * (c % 2)
    other = 1 - l
    own, yours = c * 2 + l, c * 2 + other
    is_hub = jnp.logical_and(r > 0, r < 3)

    def at(row, col, layer):
        return {"row": row, "col": col, "layer": layer}

    def arrived(ref, recv):
        pltpu.make_async_remote_copy(
            src_ref=ref, dst_ref=ref, send_sem=send_sem.at[0], recv_sem=recv,
            device_id=at(r, c, other), device_id_type=pl.DeviceIdType.MESH,
        ).wait_recv()

    def ham_rows(row, layer):
        return pl.ds(pl.multiple_of((row * 2 + layer) * depth, depth), depth)

    def chunk(j):
        return pl.ds(*spans[j])

    def piece(slot, half):
        return dbuf.at[slot, pl.ds(half * rows, rows), :]

    def ham_from(layer, j):
        first, wide = spans[j]
        return h_ref.at[:, pl.ds(pl.multiple_of(layer * cols + first, 128), wide)]

    def held(row, layer, j):
        return hbuf.at[ham_rows(row, layer), chunk(j)]

    sent = []

    def push(src, dst, recv, where):
        copy = pltpu.make_async_remote_copy(
            src_ref=src, dst_ref=dst, send_sem=send_sem.at[len(sent)], recv_sem=recv,
            device_id=where, device_id_type=pl.DeviceIdType.MESH,
        )
        copy.start()
        sent.append(copy)

    barrier = pltpu.get_barrier_semaphore()

    def greet(partners):
        for where in partners:
            pl.semaphore_signal(barrier, inc=1, device_id=where, device_id_type=pl.DeviceIdType.MESH)
        pl.semaphore_wait(barrier, len(partners))

    y = at(r, c, other)

    @pl.when(jnp.logical_not(is_hub))
    def _():
        sent.clear()
        hub = at(1 + r // 3, c, l)
        greet([hub, y])
        push(d_ref, piece(own, 1), d_sem.at[own, 1], hub)
        push(d_ref, piece(own, 1), d_sem.at[own, 1], y)
        for j in range(len(spans)):
            push(ham_from(other, j), held(r, l, j), h_sem.at[r, l, j], y)
        arrived(piece(yours, 1), d_sem.at[yours, 1])
        push(piece(yours, 1), piece(yours, 1), d_sem.at[yours, 1], hub)
        sent[0].wait_send()
        last = len(sent) - 1
        for j in range(len(spans)):
            push(ham_from(l, j), held(r, l, j), h_sem.at[r, l, j], hub)
            arrived(held(r, other, j), h_sem.at[r, other, j])
            push(held(r, other, j), held(r, other, j), h_sem.at[r, other, j], hub)
            if j == 0:
                sent[last].wait_send()
            else:
                sent[last + 2 * j - 1].wait_send()
                sent[last + 2 * j].wait_send()
        waited = {0} | set(range(last, len(sent) - 2))
        kept = []
        for j in range(len(spans)):
            arrived(ends.at[:, chunk(j)], res_sem.at[j])
            keep = pltpu.make_async_copy(ends.at[:, chunk(j)], out_ref.at[:, chunk(j)], local_sem.at[j])
            keep.start()
            kept.append(keep)
        for i, copy in enumerate(sent):
            if i not in waited:
                copy.wait_send()
        for copy in kept:
            copy.wait()

    @pl.when(is_hub)
    def _():
        sent.clear()
        end_row, far_row = 3 * r - 3, 3 - r
        far_end = 3 - end_row
        x, s = at(r, across, l), at(r, sibling, l)
        end, far = at(end_row, c, l), at(far_row, c, l)
        greet([y, x, s, end, far])

        def absorb(slot, half):
            def tile(i, _):
                at_rows = pl.ds(pl.multiple_of(half * rows + i * 128, 128), 128)
                high, low = split(dbuf[slot, at_rows, :])
                at_cols = pl.ds(pl.multiple_of(slot * width, width), width)
                dhi[at_rows, at_cols] = high
                dlo[at_rows, at_cols] = low
                return 0

            lax.fori_loop(0, rows // 128, tile, 0)

        def take(slot, half, *partners):
            arrived(piece(slot, half), d_sem.at[slot, half])
            for where in partners:
                push(piece(slot, half), piece(slot, half), d_sem.at[slot, half], where)
            absorb(slot, half)

        def straight(j):
            push(ham_from(l, j), held(r, l, j), h_sem.at[r, l, j], far)

        def relay(row, layer, j):
            arrived(held(row, layer, j), h_sem.at[row, layer, j])
            push(held(row, layer, j), held(row, layer, j), h_sem.at[row, layer, j], far)

        def relay_end(j):
            relay(end_row, l, j)
            relay(end_row, other, j)

        def split_ham(j):
            for row in (far_row, far_end):
                for layer in range(2):
                    arrived(held(row, layer, j), h_sem.at[row, layer, j])

            def part(i, _):
                at_rows = pl.ds(pl.multiple_of(i * 256, 256), 256)
                high, low = split(hbuf[at_rows, chunk(j)])
                hhi[at_rows, chunk(j)] = high
                hlo[at_rows, chunk(j)] = low
                return 0

            lax.fori_loop(0, hbuf.shape[0] // 256, part, 0)

        def rows_of(half, target, j):
            def tile(i, _):
                at_rows = pl.ds(pl.multiple_of(half * rows + i * 256, 256), 256)
                high = dhi[at_rows, :]
                total = jnp.dot(high, hhi[:, chunk(j)], preferred_element_type=jnp.float32)
                total += jnp.dot(high, hlo[:, chunk(j)], preferred_element_type=jnp.float32)
                total += jnp.dot(dlo[at_rows, :], hhi[:, chunk(j)], preferred_element_type=jnp.float32)
                target[pl.ds(pl.multiple_of(i * 256, 256), 256), chunk(j)] = total
                return 0

            lax.fori_loop(0, rows // 256, tile, 0)

        results, kept = [], []

        def end_rows(j):
            split_ham(j)
            rows_of(1, ends, j)
            copy = pltpu.make_async_remote_copy(
                src_ref=ends.at[:, chunk(j)], dst_ref=ends.at[:, chunk(j)],
                send_sem=res_send.at[j], recv_sem=res_sem.at[j],
                device_id=end, device_id_type=pl.DeviceIdType.MESH,
            )
            copy.start()
            results.append(copy)

        def own_rows(j):
            rows_of(0, mine, j)
            copy = pltpu.make_async_copy(mine.at[:, chunk(j)], out_ref.at[:, chunk(j)], local_sem.at[2 + j])
            copy.start()
            kept.append(copy)

        local_d = pltpu.make_async_copy(d_ref, piece(own, 0), local_sem.at[0])
        local_d.start()
        for where in (y, x, s):
            push(d_ref, piece(own, 0), d_sem.at[own, 0], where)
        straight(0)
        straight(1)
        for j in range(len(spans)):
            push(ham_from(other, j), held(r, l, j), h_sem.at[r, l, j], y)
        local_h = pltpu.make_async_copy(
            h_ref.at[:, pl.ds(pl.multiple_of(l * cols, cols), cols)],
            hbuf.at[ham_rows(r, l), :], local_sem.at[1],
        )
        local_h.start()
        local_d.wait()
        absorb(own, 0)
        take(own, 1, x, s)
        relay(r, other, 0)
        relay(r, other, 1)
        straight(2)
        take(yours, 1, x, s)
        relay(r, other, 2)
        straight(3)
        take(yours, 0, x, s)
        relay_end(0)
        take(across * 2 + l, 1, s)
        relay(r, other, 3)
        relay_end(1)
        take(across * 2 + other, 1, s)
        straight(4)
        relay(r, other, 4)
        away = (sibling + 2) % 4
        beside = [col * 2 + layer for col in (sibling, away) for layer in (l, other)]
        for slot in beside:
            take(slot, 1)
        local_h.wait()
        end_rows(0)
        take(across * 2 + l, 0, s)
        take(across * 2 + other, 0, s)
        relay_end(2)
        end_rows(1)
        relay_end(3)
        for slot in beside:
            take(slot, 0)
        own_rows(0)
        relay_end(4)
        own_rows(1)
        for j in range(2, len(spans)):
            end_rows(j)
            own_rows(j)
        for copy in sent + results:
            copy.wait_send()
        for copy in kept:
            copy.wait()


def chunk_spans(cols):
    quarter = cols // 4
    widths = [quarter] * 3 + [quarter // 2] * 2
    return [(sum(widths[:j]), width) for j, width in enumerate(widths)]


def product_of(dens, ham, layers, grid_cols):
    rows, width = dens.shape
    depth, ham_cols = ham.shape
    cols = ham_cols // layers
    inner = layers * grid_cols * width
    chunks = len(chunk_spans(cols))
    f32, bf16 = jnp.float32, jnp.bfloat16
    dma = pltpu.SemaphoreType.DMA
    return pl.pallas_call(
        kernel,
        out_shape=jax.ShapeDtypeStruct((rows, cols), f32),
        in_specs=[pl.BlockSpec(memory_space=pl.ANY)] * 2,
        out_specs=pl.BlockSpec(memory_space=pl.ANY),
        scratch_shapes=[
            pltpu.VMEM((layers * grid_cols, 2 * rows, width), f32),
            pltpu.VMEM((inner, cols), f32),
            pltpu.VMEM((2 * rows, inner), bf16),
            pltpu.VMEM((2 * rows, inner), bf16),
            pltpu.VMEM((inner, cols), bf16),
            pltpu.VMEM((inner, cols), bf16),
            pltpu.VMEM((rows, cols), f32),
            pltpu.VMEM((rows, cols), f32),
            dma((layers * grid_cols, 2)),
            dma((4, 2, chunks)),
            dma((chunks,)),
            dma((16 + 5 * chunks,)),
            dma((chunks,)),
            dma((2 + chunks,)),
        ],
        compiler_params=pltpu.CompilerParams(
            collective_id=0, has_side_effects=True, vmem_limit_bytes=52 * 2**20
        ),
    )(dens, ham)


def lined_up(density, dens_mask, hamiltonian, ham_mask, filter_mask, *, layers, grid_cols):
    dens = density[0] * expand(dens_mask[0])
    ham = masked_ham(hamiltonian, ham_mask)
    total = product_of(dens, ham, layers, grid_cols)
    kept_blocks = filter_mask.shape[1] // layers
    kept = lax.dynamic_slice_in_dim(filter_mask, lax.axis_index("layer") * kept_blocks, kept_blocks, 1)
    wide = jnp.repeat(kept.astype(jnp.float32), BLOCK, axis=1)
    out = total.reshape(-1, BLOCK, total.shape[1]) * wide[:, None, :]
    return out.reshape(total.shape)


def gathered(density, dens_mask, hamiltonian, ham_mask, filter_mask):
    dens = lax.all_gather(density * expand(dens_mask), "col", axis=2, tiled=True)[0]
    ham = lax.all_gather(masked_ham(hamiltonian, ham_mask), "row", axis=0, tiled=True)
    part = jnp.dot(dens, ham, precision=lax.Precision.HIGHEST, preferred_element_type=jnp.float32)
    return lax.psum_scatter(part * expand(filter_mask), "layer", scatter_dimension=1, tiled=True)


def solution(mesh):
    sizes = dict(mesh.shape)
    layers, grid_cols = sizes["layer"], sizes["col"]
    body = gathered
    if sizes == {"row": 4, "col": 4, "layer": 2}:
        body = functools.partial(lined_up, layers=layers, grid_cols=grid_cols)
    return jax.shard_map(
        body,
        mesh=mesh,
        in_specs=(
            P("layer", "row", "col"),
            P("layer", "row", "col"),
            P("layer", "row", "col"),
            P("layer", None, "col"),
            P("row", "col"),
        ),
        out_specs=P("row", ("col", "layer")),
        check_vma=False,
    )
```

```python
import functools

import jax
import jax.numpy as jnp
from jax import lax
from jax.experimental import pallas as pl
from jax.experimental.pallas import tpu as pltpu
from jax.sharding import PartitionSpec as P

BLOCK = 64


def expand(block_mask):
    widened = jnp.repeat(block_mask.astype(jnp.float32), BLOCK, axis=-2)
    return jnp.repeat(widened, BLOCK, axis=-1)


def masked_ham(hamiltonian, ham_mask):
    blocks = hamiltonian.shape[1] // BLOCK
    mine = lax.dynamic_slice_in_dim(ham_mask[0], lax.axis_index("row") * blocks, blocks, 0)
    wide = jnp.repeat(mine.astype(jnp.float32), BLOCK, axis=1)
    ham = hamiltonian[0].reshape(blocks, BLOCK, -1) * wide[:, None, :]
    return ham.reshape(hamiltonian.shape[1:])


def split(x):
    high = x.astype(jnp.bfloat16)
    return high, (x - high.astype(jnp.float32)).astype(jnp.bfloat16)


def kernel(
    d_ref, h_ref, out_ref,
    dbuf, hbuf, dhi, dlo, hhi, hlo, mine, ends,
    d_sem, h_sem, res_sem, send_sem, res_send, local_sem,
):
    r, c, l = lax.axis_index("row"), lax.axis_index("col"), lax.axis_index("layer")
    rows, width = d_ref.shape
    depth = h_ref.shape[0]
    cols = out_ref.shape[1]
    spans = chunk_spans(cols)
    across = (c + 2) % 4
    sibling = c + 1 - 2 * (c % 2)
    other = 1 - l
    own, yours = c * 2 + l, c * 2 + other
    is_hub = jnp.logical_and(r > 0, r < 3)

    def at(row, col, layer):
        return {"row": row, "col": col, "layer": layer}

    def arrived(ref, recv):
        pltpu.make_async_remote_copy(
            src_ref=ref, dst_ref=ref, send_sem=send_sem.at[0], recv_sem=recv,
            device_id=at(r, c, other), device_id_type=pl.DeviceIdType.MESH,
        ).wait_recv()

    def ham_rows(row, layer):
        return pl.ds(pl.multiple_of((row * 2 + layer) * depth, depth), depth)

    def chunk(j):
        return pl.ds(*spans[j])

    def piece(slot, half):
        return dbuf.at[slot, pl.ds(half * rows, rows), :]

    def ham_from(layer, j):
        first, wide = spans[j]
        return h_ref.at[:, pl.ds(pl.multiple_of(layer * cols + first, 128), wide)]

    def held(row, layer, j):
        return hbuf.at[ham_rows(row, layer), chunk(j)]

    sent = []

    def push(src, dst, recv, where):
        copy = pltpu.make_async_remote_copy(
            src_ref=src, dst_ref=dst, send_sem=send_sem.at[len(sent)], recv_sem=recv,
            device_id=where, device_id_type=pl.DeviceIdType.MESH,
        )
        copy.start()
        sent.append(copy)

    barrier = pltpu.get_barrier_semaphore()

    def greet(partners):
        for where in partners:
            pl.semaphore_signal(barrier, inc=1, device_id=where, device_id_type=pl.DeviceIdType.MESH)
        pl.semaphore_wait(barrier, len(partners))

    y = at(r, c, other)

    @pl.when(jnp.logical_not(is_hub))
    def _():
        sent.clear()
        hub = at(1 + r // 3, c, l)
        greet([hub, y])
        push(d_ref, piece(own, 1), d_sem.at[own, 1], hub)
        push(d_ref, piece(own, 1), d_sem.at[own, 1], y)
        for j in range(len(spans)):
            push(ham_from(other, j), held(r, l, j), h_sem.at[r, l, j], y)
        arrived(piece(yours, 1), d_sem.at[yours, 1])
        push(piece(yours, 1), piece(yours, 1), d_sem.at[yours, 1], hub)
        sent[0].wait_send()
        last = len(sent) - 1
        for j in range(len(spans)):
            push(ham_from(l, j), held(r, l, j), h_sem.at[r, l, j], hub)
            arrived(held(r, other, j), h_sem.at[r, other, j])
            push(held(r, other, j), held(r, other, j), h_sem.at[r, other, j], hub)
            if j == 0:
                sent[last].wait_send()
            else:
                sent[last + 2 * j - 1].wait_send()
                sent[last + 2 * j].wait_send()
        waited = {0} | set(range(last, len(sent) - 2))
        kept = []
        for j in range(len(spans)):
            arrived(ends.at[:, chunk(j)], res_sem.at[j])
            keep = pltpu.make_async_copy(ends.at[:, chunk(j)], out_ref.at[:, chunk(j)], local_sem.at[j])
            keep.start()
            kept.append(keep)
        for i, copy in enumerate(sent):
            if i not in waited:
                copy.wait_send()
        for copy in kept:
            copy.wait()

    @pl.when(is_hub)
    def _():
        sent.clear()
        end_row, far_row = 3 * r - 3, 3 - r
        far_end = 3 - end_row
        x, s = at(r, across, l), at(r, sibling, l)
        end, far = at(end_row, c, l), at(far_row, c, l)
        greet([y, x, s, end, far])

        def absorb(slot, half):
            def tile(i, _):
                at_rows = pl.ds(pl.multiple_of(half * rows + i * 128, 128), 128)
                high, low = split(dbuf[slot, at_rows, :])
                at_cols = pl.ds(pl.multiple_of(slot * width, width), width)
                dhi[at_rows, at_cols] = high
                dlo[at_rows, at_cols] = low
                return 0

            lax.fori_loop(0, rows // 128, tile, 0)

        def take(slot, half, *partners):
            arrived(piece(slot, half), d_sem.at[slot, half])
            for where in partners:
                push(piece(slot, half), piece(slot, half), d_sem.at[slot, half], where)
            absorb(slot, half)

        def straight(j):
            push(ham_from(l, j), held(r, l, j), h_sem.at[r, l, j], far)

        def relay(row, layer, j):
            arrived(held(row, layer, j), h_sem.at[row, layer, j])
            push(held(row, layer, j), held(row, layer, j), h_sem.at[row, layer, j], far)

        def relay_end(j):
            relay(end_row, l, j)
            relay(end_row, other, j)

        def split_ham(j):
            for row in (far_row, far_end):
                for layer in range(2):
                    arrived(held(row, layer, j), h_sem.at[row, layer, j])

            def part(i, _):
                at_rows = pl.ds(pl.multiple_of(i * 256, 256), 256)
                high, low = split(hbuf[at_rows, chunk(j)])
                hhi[at_rows, chunk(j)] = high
                hlo[at_rows, chunk(j)] = low
                return 0

            lax.fori_loop(0, hbuf.shape[0] // 256, part, 0)

        def rows_of(half, target, j):
            def tile(i, _):
                at_rows = pl.ds(pl.multiple_of(half * rows + i * 256, 256), 256)
                high = dhi[at_rows, :]
                total = jnp.dot(high, hhi[:, chunk(j)], preferred_element_type=jnp.float32)
                total += jnp.dot(high, hlo[:, chunk(j)], preferred_element_type=jnp.float32)
                total += jnp.dot(dlo[at_rows, :], hhi[:, chunk(j)], preferred_element_type=jnp.float32)
                target[pl.ds(pl.multiple_of(i * 256, 256), 256), chunk(j)] = total
                return 0

            lax.fori_loop(0, rows // 256, tile, 0)

        results, kept = [], []

        def end_rows(j):
            split_ham(j)
            rows_of(1, ends, j)
            copy = pltpu.make_async_remote_copy(
                src_ref=ends.at[:, chunk(j)], dst_ref=ends.at[:, chunk(j)],
                send_sem=res_send.at[j], recv_sem=res_sem.at[j],
                device_id=end, device_id_type=pl.DeviceIdType.MESH,
            )
            copy.start()
            results.append(copy)

        def own_rows(j):
            rows_of(0, mine, j)
            copy = pltpu.make_async_copy(mine.at[:, chunk(j)], out_ref.at[:, chunk(j)], local_sem.at[2 + j])
            copy.start()
            kept.append(copy)

        local_d = pltpu.make_async_copy(d_ref, piece(own, 0), local_sem.at[0])
        local_d.start()
        for where in (y, x, s):
            push(d_ref, piece(own, 0), d_sem.at[own, 0], where)
        straight(0)
        straight(1)
        for j in range(len(spans)):
            push(ham_from(other, j), held(r, l, j), h_sem.at[r, l, j], y)
        local_h = pltpu.make_async_copy(
            h_ref.at[:, pl.ds(pl.multiple_of(l * cols, cols), cols)],
            hbuf.at[ham_rows(r, l), :], local_sem.at[1],
        )
        local_h.start()
        local_d.wait()
        absorb(own, 0)
        take(own, 1, x, s)
        relay(r, other, 0)
        relay(r, other, 1)
        straight(2)
        take(yours, 1, x, s)
        relay(r, other, 2)
        take(yours, 0, x, s)
        relay_end(0)
        take(across * 2 + l, 1, s)
        straight(3)
        relay_end(1)
        take(across * 2 + other, 1, s)
        relay(r, other, 3)
        away = (sibling + 2) % 4
        beside = [col * 2 + layer for col in (sibling, away) for layer in (l, other)]
        for slot in beside:
            take(slot, 1)
        local_h.wait()
        end_rows(0)
        relay_end(2)
        take(across * 2 + l, 0, s)
        take(across * 2 + other, 0, s)
        end_rows(1)
        relay_end(3)
        straight(4)
        relay(r, other, 4)
        for slot in beside:
            take(slot, 0)
        own_rows(0)
        relay_end(4)
        own_rows(1)
        end_rows(2)
        own_rows(2)
        end_rows(3)
        end_rows(4)
        own_rows(3)
        own_rows(4)
        for copy in sent + results:
            copy.wait_send()
        for copy in kept:
            copy.wait()


def chunk_spans(cols):
    quarter = cols // 4
    widths = [quarter] * 3 + [quarter // 2] * 2
    return [(sum(widths[:j]), width) for j, width in enumerate(widths)]


def product_of(dens, ham, layers, grid_cols):
    rows, width = dens.shape
    depth, ham_cols = ham.shape
    cols = ham_cols // layers
    inner = layers * grid_cols * width
    chunks = len(chunk_spans(cols))
    f32, bf16 = jnp.float32, jnp.bfloat16
    dma = pltpu.SemaphoreType.DMA
    return pl.pallas_call(
        kernel,
        out_shape=jax.ShapeDtypeStruct((rows, cols), f32),
        in_specs=[pl.BlockSpec(memory_space=pl.ANY)] * 2,
        out_specs=pl.BlockSpec(memory_space=pl.ANY),
        scratch_shapes=[
            pltpu.VMEM((layers * grid_cols, 2 * rows, width), f32),
            pltpu.VMEM((inner, cols), f32),
            pltpu.VMEM((2 * rows, inner), bf16),
            pltpu.VMEM((2 * rows, inner), bf16),
            pltpu.VMEM((inner, cols), bf16),
            pltpu.VMEM((inner, cols), bf16),
            pltpu.VMEM((rows, cols), f32),
            pltpu.VMEM((rows, cols), f32),
            dma((layers * grid_cols, 2)),
            dma((4, 2, chunks)),
            dma((chunks,)),
            dma((16 + 5 * chunks,)),
            dma((chunks,)),
            dma((2 + chunks,)),
        ],
        compiler_params=pltpu.CompilerParams(
            collective_id=0, has_side_effects=True, vmem_limit_bytes=52 * 2**20
        ),
    )(dens, ham)


def lined_up(density, dens_mask, hamiltonian, ham_mask, filter_mask, *, layers, grid_cols):
    dens = density[0] * expand(dens_mask[0])
    ham = masked_ham(hamiltonian, ham_mask)
    total = product_of(dens, ham, layers, grid_cols)
    kept_blocks = filter_mask.shape[1] // layers
    kept = lax.dynamic_slice_in_dim(filter_mask, lax.axis_index("layer") * kept_blocks, kept_blocks, 1)
    wide = jnp.repeat(kept.astype(jnp.float32), BLOCK, axis=1)
    out = total.reshape(-1, BLOCK, total.shape[1]) * wide[:, None, :]
    return out.reshape(total.shape)


def gathered(density, dens_mask, hamiltonian, ham_mask, filter_mask):
    dens = lax.all_gather(density * expand(dens_mask), "col", axis=2, tiled=True)[0]
    ham = lax.all_gather(masked_ham(hamiltonian, ham_mask), "row", axis=0, tiled=True)
    part = jnp.dot(dens, ham, precision=lax.Precision.HIGHEST, preferred_element_type=jnp.float32)
    return lax.psum_scatter(part * expand(filter_mask), "layer", scatter_dimension=1, tiled=True)


def solution(mesh):
    sizes = dict(mesh.shape)
    layers, grid_cols = sizes["layer"], sizes["col"]
    body = gathered
    if sizes == {"row": 4, "col": 4, "layer": 2}:
        body = functools.partial(lined_up, layers=layers, grid_cols=grid_cols)
    return jax.shard_map(
        body,
        mesh=mesh,
        in_specs=(
            P("layer", "row", "col"),
            P("layer", "row", "col"),
            P("layer", "row", "col"),
            P("layer", None, "col"),
            P("row", "col"),
        ),
        out_specs=P("row", ("col", "layer")),
        check_vma=False,
    )
```

```python
import functools

import jax
import jax.numpy as jnp
from jax import lax
from jax.experimental import pallas as pl
from jax.experimental.pallas import tpu as pltpu
from jax.sharding import PartitionSpec as P

BLOCK = 64


def expand(block_mask):
    widened = jnp.repeat(block_mask.astype(jnp.float32), BLOCK, axis=-2)
    return jnp.repeat(widened, BLOCK, axis=-1)


def masked_ham(hamiltonian, ham_mask):
    blocks = hamiltonian.shape[1] // BLOCK
    mine = lax.dynamic_slice_in_dim(ham_mask[0], lax.axis_index("row") * blocks, blocks, 0)
    wide = jnp.repeat(mine.astype(jnp.float32), BLOCK, axis=1)
    ham = hamiltonian[0].reshape(blocks, BLOCK, -1) * wide[:, None, :]
    return ham.reshape(hamiltonian.shape[1:])


def split(x):
    high = x.astype(jnp.bfloat16)
    return high, (x - high.astype(jnp.float32)).astype(jnp.bfloat16)


def kernel(
    d_ref, d_mask, h_ref, h_mask, out_ref,
    dbuf, hbuf, masks, dhi, dlo, hhi, hlo, mine, ends,
    d_sem, h_sem, res_sem, send_sem, res_send, local_sem, mask_sem,
):
    r, c, l = lax.axis_index("row"), lax.axis_index("col"), lax.axis_index("layer")
    rows, width = d_ref.shape
    depth = h_ref.shape[0]
    cols = out_ref.shape[1]
    spans = chunk_spans(cols)
    across = (c + 2) % 4
    sibling = c + 1 - 2 * (c % 2)
    other = 1 - l
    own, yours = c * 2 + l, c * 2 + other
    is_hub = jnp.logical_and(r > 0, r < 3)

    def at(row, col, layer):
        return {"row": row, "col": col, "layer": layer}

    def arrived(ref, recv):
        pltpu.make_async_remote_copy(
            src_ref=ref, dst_ref=ref, send_sem=send_sem.at[0], recv_sem=recv,
            device_id=at(r, c, other), device_id_type=pl.DeviceIdType.MESH,
        ).wait_recv()

    def ham_rows(row, layer):
        return pl.ds(pl.multiple_of((row * 2 + layer) * depth, depth), depth)

    def chunk(j):
        return pl.ds(*spans[j])

    def piece(slot, half):
        return dbuf.at[slot, pl.ds(half * rows, rows), :]

    def ham_from(layer, j):
        first, wide = spans[j]
        return h_ref.at[:, pl.ds(pl.multiple_of(layer * cols + first, 128), wide)]

    def held(row, layer, j):
        return hbuf.at[ham_rows(row, layer), chunk(j)]

    sent = []

    def push(src, dst, recv, where):
        copy = pltpu.make_async_remote_copy(
            src_ref=src, dst_ref=dst, send_sem=send_sem.at[len(sent)], recv_sem=recv,
            device_id=where, device_id_type=pl.DeviceIdType.MESH,
        )
        copy.start()
        sent.append(copy)

    barrier = pltpu.get_barrier_semaphore()

    def greet(partners):
        for where in partners:
            pl.semaphore_signal(barrier, inc=1, device_id=where, device_id_type=pl.DeviceIdType.MESH)
        pl.semaphore_wait(barrier, len(partners))

    def mask_dens(half):
        for i in range(rows // BLOCK):
            block = pl.ds(half * rows + i * BLOCK, BLOCK)
            dbuf[own, block, :] = d_ref[pl.ds(i * BLOCK, BLOCK), :] * d_mask[pl.ds(i, 1), :]

    y = at(r, c, other)

    @pl.when(jnp.logical_not(is_hub))
    def _():
        sent.clear()
        hub = at(1 + r // 3, c, l)
        mask_dens(1)
        greet([hub, y])
        push(piece(own, 1), piece(own, 1), d_sem.at[own, 1], hub)
        push(piece(own, 1), piece(own, 1), d_sem.at[own, 1], y)
        for j in range(len(spans)):
            push(ham_from(other, j), held(r, l, j), h_sem.at[r, l, j], y)
        arrived(piece(yours, 1), d_sem.at[yours, 1])
        push(piece(yours, 1), piece(yours, 1), d_sem.at[yours, 1], hub)
        sent[0].wait_send()
        last = len(sent) - 1
        for j in range(len(spans)):
            push(ham_from(l, j), held(r, l, j), h_sem.at[r, l, j], hub)
            arrived(held(r, other, j), h_sem.at[r, other, j])
            push(held(r, other, j), held(r, other, j), h_sem.at[r, other, j], hub)
            if j == 0:
                sent[last].wait_send()
            else:
                sent[last + 2 * j - 1].wait_send()
                sent[last + 2 * j].wait_send()
        waited = {0} | set(range(last, len(sent) - 2))
        kept = []
        for j in range(len(spans)):
            arrived(ends.at[:, chunk(j)], res_sem.at[j])
            keep = pltpu.make_async_copy(ends.at[:, chunk(j)], out_ref.at[:, chunk(j)], local_sem.at[j])
            keep.start()
            kept.append(keep)
        for i, copy in enumerate(sent):
            if i not in waited:
                copy.wait_send()
        for copy in kept:
            copy.wait()

    @pl.when(is_hub)
    def _():
        sent.clear()
        end_row, far_row = 3 * r - 3, 3 - r
        far_end = 3 - end_row
        x, s = at(r, across, l), at(r, sibling, l)
        end, far = at(end_row, c, l), at(far_row, c, l)
        mask_dens(0)
        greet([y, x, s, end, far])

        def absorb(slot, half):
            def tile(i, _):
                at_rows = pl.ds(pl.multiple_of(half * rows + i * 128, 128), 128)
                high, low = split(dbuf[slot, at_rows, :])
                at_cols = pl.ds(pl.multiple_of(slot * width, width), width)
                dhi[at_rows, at_cols] = high
                dlo[at_rows, at_cols] = low
                return 0

            lax.fori_loop(0, rows // 128, tile, 0)

        def take(slot, half, *partners):
            arrived(piece(slot, half), d_sem.at[slot, half])
            for where in partners:
                push(piece(slot, half), piece(slot, half), d_sem.at[slot, half], where)
            absorb(slot, half)

        def mask_from(layer):
            return h_mask.at[:, :, pl.ds(pl.multiple_of(layer * cols, cols), cols)]

        def straight(j):
            push(ham_from(l, j), held(r, l, j), h_sem.at[r, l, j], far)

        def relay(row, layer, j):
            arrived(held(row, layer, j), h_sem.at[row, layer, j])
            push(held(row, layer, j), held(row, layer, j), h_sem.at[row, layer, j], far)

        def relay_end(j):
            relay(end_row, l, j)
            relay(end_row, other, j)

        def split_ham(j):
            for row in (far_row, far_end):
                for layer in range(2):
                    arrived(held(row, layer, j), h_sem.at[row, layer, j])

            def part(i, _):
                kept_blocks = masks[i // 2, i % 2, :, chunk(j)]
                for k in range(depth // BLOCK):
                    at_rows = pl.ds(pl.multiple_of(i * depth + k * BLOCK, BLOCK), BLOCK)
                    high, low = split(hbuf[at_rows, chunk(j)] * kept_blocks[k : k + 1, :])
                    hhi[at_rows, chunk(j)] = high
                    hlo[at_rows, chunk(j)] = low
                return 0

            lax.fori_loop(0, hbuf.shape[0] // depth, part, 0)

        def rows_of(half, target, j):
            def tile(i, _):
                at_rows = pl.ds(pl.multiple_of(half * rows + i * 256, 256), 256)
                high = dhi[at_rows, :]
                total = jnp.dot(high, hhi[:, chunk(j)], preferred_element_type=jnp.float32)
                total += jnp.dot(high, hlo[:, chunk(j)], preferred_element_type=jnp.float32)
                total += jnp.dot(dlo[at_rows, :], hhi[:, chunk(j)], preferred_element_type=jnp.float32)
                target[pl.ds(pl.multiple_of(i * 256, 256), 256), chunk(j)] = total
                return 0

            lax.fori_loop(0, rows // 256, tile, 0)

        results, kept = [], []

        def end_rows(j):
            split_ham(j)
            rows_of(1, ends, j)
            copy = pltpu.make_async_remote_copy(
                src_ref=ends.at[:, chunk(j)], dst_ref=ends.at[:, chunk(j)],
                send_sem=res_send.at[j], recv_sem=res_sem.at[j],
                device_id=end, device_id_type=pl.DeviceIdType.MESH,
            )
            copy.start()
            results.append(copy)

        def own_rows(j):
            rows_of(0, mine, j)
            copy = pltpu.make_async_copy(mine.at[:, chunk(j)], out_ref.at[:, chunk(j)], local_sem.at[2 + j])
            copy.start()
            kept.append(copy)

        for where in (y, x, s):
            push(piece(own, 0), piece(own, 0), d_sem.at[own, 0], where)
        straight(0)
        straight(1)
        for j in range(len(spans)):
            push(ham_from(other, j), held(r, l, j), h_sem.at[r, l, j], y)
        local_h = pltpu.make_async_copy(
            h_ref.at[:, pl.ds(pl.multiple_of(l * cols, cols), cols)],
            hbuf.at[ham_rows(r, l), :], local_sem.at[1],
        )
        local_h.start()
        push(mask_from(other), masks.at[:, l], mask_sem, y)
        local_mask = pltpu.make_async_copy(mask_from(l), masks.at[:, l], local_sem.at[0])
        local_mask.start()
        absorb(own, 0)
        take(own, 1, x, s)
        relay(r, other, 0)
        relay(r, other, 1)
        straight(2)
        take(yours, 1, x, s)
        relay(r, other, 2)
        take(yours, 0, x, s)
        relay_end(0)
        take(across * 2 + l, 1, s)
        straight(3)
        relay_end(1)
        take(across * 2 + other, 1, s)
        relay(r, other, 3)
        away = (sibling + 2) % 4
        beside = [col * 2 + layer for col in (sibling, away) for layer in (l, other)]
        for slot in beside:
            take(slot, 1)
        local_h.wait()
        local_mask.wait()
        arrived(masks.at[:, other], mask_sem)
        end_rows(0)
        relay_end(2)
        take(across * 2 + l, 0, s)
        take(across * 2 + other, 0, s)
        end_rows(1)
        relay_end(3)
        straight(4)
        relay(r, other, 4)
        for slot in beside:
            take(slot, 0)
        own_rows(0)
        relay_end(4)
        own_rows(1)
        end_rows(2)
        own_rows(2)
        end_rows(3)
        end_rows(4)
        own_rows(3)
        own_rows(4)
        for copy in sent + results:
            copy.wait_send()
        for copy in kept:
            copy.wait()


def chunk_spans(cols):
    quarter = cols // 4
    widths = [quarter] * 3 + [quarter // 2] * 2
    return [(sum(widths[:j]), width) for j, width in enumerate(widths)]


def product_of(dens, dens_wide, ham, ham_wide, layers, grid_cols):
    rows, width = dens.shape
    depth, ham_cols = ham.shape
    cols = ham_cols // layers
    inner = layers * grid_cols * width
    chunks = len(chunk_spans(cols))
    f32, bf16 = jnp.float32, jnp.bfloat16
    dma = pltpu.SemaphoreType.DMA
    return pl.pallas_call(
        kernel,
        out_shape=jax.ShapeDtypeStruct((rows, cols), f32),
        in_specs=[
            pl.BlockSpec(memory_space=pltpu.VMEM),
            pl.BlockSpec(memory_space=pltpu.VMEM),
            pl.BlockSpec(memory_space=pl.ANY),
            pl.BlockSpec(memory_space=pltpu.VMEM),
        ],
        out_specs=pl.BlockSpec(memory_space=pl.ANY),
        scratch_shapes=[
            pltpu.VMEM((layers * grid_cols, 2 * rows, width), f32),
            pltpu.VMEM((inner, cols), f32),
            pltpu.VMEM((ham_wide.shape[0], layers, ham_wide.shape[1], cols), f32),
            pltpu.VMEM((2 * rows, inner), bf16),
            pltpu.VMEM((2 * rows, inner), bf16),
            pltpu.VMEM((inner, cols), bf16),
            pltpu.VMEM((inner, cols), bf16),
            pltpu.VMEM((rows, cols), f32),
            pltpu.VMEM((rows, cols), f32),
            dma((layers * grid_cols, 2)),
            dma((4, 2, chunks)),
            dma((chunks,)),
            dma((16 + 5 * chunks,)),
            dma((chunks,)),
            dma((2 + chunks,)),
            dma,
        ],
        compiler_params=pltpu.CompilerParams(
            collective_id=0, has_side_effects=True, vmem_limit_bytes=52 * 2**20
        ),
    )(dens, dens_wide, ham, ham_wide)


def lined_up(density, dens_mask, hamiltonian, ham_mask, filter_mask, *, layers, grid_cols):
    dens_wide = jnp.repeat(dens_mask[0].astype(jnp.float32), BLOCK, axis=1)
    ham_wide = jnp.repeat(ham_mask[0].astype(jnp.float32), BLOCK, axis=1)
    ham_wide = ham_wide.reshape(-1, hamiltonian.shape[1] // BLOCK, hamiltonian.shape[2])
    total = product_of(density[0], dens_wide, hamiltonian[0], ham_wide, layers, grid_cols)
    kept_blocks = filter_mask.shape[1] // layers
    kept = lax.dynamic_slice_in_dim(filter_mask, lax.axis_index("layer") * kept_blocks, kept_blocks, 1)
    wide = jnp.repeat(kept.astype(jnp.float32), BLOCK, axis=1)
    out = total.reshape(-1, BLOCK, total.shape[1]) * wide[:, None, :]
    return out.reshape(total.shape)


def gathered(density, dens_mask, hamiltonian, ham_mask, filter_mask):
    dens = lax.all_gather(density * expand(dens_mask), "col", axis=2, tiled=True)[0]
    ham = lax.all_gather(masked_ham(hamiltonian, ham_mask), "row", axis=0, tiled=True)
    part = jnp.dot(dens, ham, precision=lax.Precision.HIGHEST, preferred_element_type=jnp.float32)
    return lax.psum_scatter(part * expand(filter_mask), "layer", scatter_dimension=1, tiled=True)


def solution(mesh):
    sizes = dict(mesh.shape)
    layers, grid_cols = sizes["layer"], sizes["col"]
    body = gathered
    if sizes == {"row": 4, "col": 4, "layer": 2}:
        body = functools.partial(lined_up, layers=layers, grid_cols=grid_cols)
    return jax.shard_map(
        body,
        mesh=mesh,
        in_specs=(
            P("layer", "row", "col"),
            P("layer", "row", "col"),
            P("layer", "row", "col"),
            P("layer", None, "col"),
            P("row", "col"),
        ),
        out_specs=P("row", ("col", "layer")),
        check_vma=False,
    )
```

```python
import functools

import jax
import jax.numpy as jnp
from jax import lax
from jax.experimental import pallas as pl
from jax.experimental.pallas import tpu as pltpu
from jax.sharding import PartitionSpec as P

BLOCK = 64


def expand(block_mask):
    widened = jnp.repeat(block_mask.astype(jnp.float32), BLOCK, axis=-2)
    return jnp.repeat(widened, BLOCK, axis=-1)


def masked_ham(hamiltonian, ham_mask):
    blocks = hamiltonian.shape[1] // BLOCK
    mine = lax.dynamic_slice_in_dim(ham_mask[0], lax.axis_index("row") * blocks, blocks, 0)
    wide = jnp.repeat(mine.astype(jnp.float32), BLOCK, axis=1)
    ham = hamiltonian[0].reshape(blocks, BLOCK, -1) * wide[:, None, :]
    return ham.reshape(hamiltonian.shape[1:])


def split(x):
    high = x.astype(jnp.bfloat16)
    return high, (x - high.astype(jnp.float32)).astype(jnp.bfloat16)


def kernel(
    d_ref, d_mask, h_ref, h_mask, out_ref,
    dbuf, hbuf, raw, masks, yours_mask, dhi, dlo, hhi, hlo, ends,
    d_sem, h_sem, res_sem, send_sem, res_send, local_sem, mask_sem,
):
    r, c, l = lax.axis_index("row"), lax.axis_index("col"), lax.axis_index("layer")
    rows, width = d_ref.shape
    depth = h_ref.shape[0]
    cols = out_ref.shape[1]
    spans = chunk_spans(cols)
    across = (c + 2) % 4
    sibling = c + 1 - 2 * (c % 2)
    other = 1 - l
    own, yours = c * 2 + l, c * 2 + other
    is_hub = jnp.logical_and(r > 0, r < 3)

    def at(row, col, layer):
        return {"row": row, "col": col, "layer": layer}

    def arrived(ref, recv):
        pltpu.make_async_remote_copy(
            src_ref=ref, dst_ref=ref, send_sem=send_sem.at[0], recv_sem=recv,
            device_id=at(r, c, other), device_id_type=pl.DeviceIdType.MESH,
        ).wait_recv()

    def ham_rows(row, layer):
        return pl.ds(pl.multiple_of((row * 2 + layer) * depth, depth), depth)

    def chunk(j):
        return pl.ds(*spans[j])

    def piece(slot, half):
        return dbuf.at[slot, pl.ds(half * rows, rows), :]

    def ham_from(layer, j):
        first, wide = spans[j]
        return h_ref.at[:, pl.ds(pl.multiple_of(layer * cols + first, 128), wide)]

    def held(row, layer, j):
        return hbuf.at[ham_rows(row, layer), chunk(j)]

    sent = []

    def push(src, dst, recv, where):
        copy = pltpu.make_async_remote_copy(
            src_ref=src, dst_ref=dst, send_sem=send_sem.at[len(sent)], recv_sem=recv,
            device_id=where, device_id_type=pl.DeviceIdType.MESH,
        )
        copy.start()
        sent.append(copy)

    barrier = pltpu.get_barrier_semaphore()

    def greet(partners):
        for where in partners:
            pl.semaphore_signal(barrier, inc=1, device_id=where, device_id_type=pl.DeviceIdType.MESH)
        pl.semaphore_wait(barrier, len(partners))

    def mask_dens(half):
        load.wait()
        for i in range(rows // BLOCK):
            block = pl.ds(half * rows + i * BLOCK, BLOCK)
            dbuf[own, block, :] = raw[pl.ds(i * BLOCK, BLOCK), :] * d_mask[pl.ds(i, 1), :]

    y = at(r, c, other)
    load = pltpu.make_async_copy(d_ref, raw, local_sem.at[0])
    load.start()

    @pl.when(jnp.logical_not(is_hub))
    def _():
        sent.clear()
        hub = at(1 + r // 3, c, l)
        greet([hub, y])
        push(ham_from(other, 0), held(r, l, 0), h_sem.at[r, l, 0], y)
        mask_dens(1)
        push(piece(own, 1), piece(own, 1), d_sem.at[own, 1], hub)
        push(piece(own, 1), piece(own, 1), d_sem.at[own, 1], y)
        for j in range(1, len(spans)):
            push(ham_from(other, j), held(r, l, j), h_sem.at[r, l, j], y)
        arrived(piece(yours, 1), d_sem.at[yours, 1])
        push(piece(yours, 1), piece(yours, 1), d_sem.at[yours, 1], hub)
        sent[1].wait_send()
        last = len(sent) - 1
        for j in range(len(spans)):
            push(ham_from(l, j), held(r, l, j), h_sem.at[r, l, j], hub)
            arrived(held(r, other, j), h_sem.at[r, other, j])
            push(held(r, other, j), held(r, other, j), h_sem.at[r, other, j], hub)
            if j == 0:
                sent[last].wait_send()
            else:
                sent[last + 2 * j - 1].wait_send()
                sent[last + 2 * j].wait_send()
        waited = {1} | set(range(last, len(sent) - 2))
        for j in range(len(spans)):
            arrived(ends.at[:, chunk(j)], res_sem.at[j])
            out_ref[:, chunk(j)] = ends[:, chunk(j)]
        for i, copy in enumerate(sent):
            if i not in waited:
                copy.wait_send()

    @pl.when(is_hub)
    def _():
        sent.clear()
        end_row, far_row = 3 * r - 3, 3 - r
        far_end = 3 - end_row
        x, s = at(r, across, l), at(r, sibling, l)
        end, far = at(end_row, c, l), at(far_row, c, l)
        greet([y, x, s, end, far])

        def absorb(slot, half):
            def tile(i, _):
                at_rows = pl.ds(pl.multiple_of(half * rows + i * 128, 128), 128)
                high, low = split(dbuf[slot, at_rows, :])
                at_cols = pl.ds(pl.multiple_of(slot * width, width), width)
                dhi[at_rows, at_cols] = high
                dlo[at_rows, at_cols] = low
                return 0

            lax.fori_loop(0, rows // 128, tile, 0)

        def take(slot, half, *partners):
            arrived(piece(slot, half), d_sem.at[slot, half])
            for where in partners:
                push(piece(slot, half), piece(slot, half), d_sem.at[slot, half], where)
            absorb(slot, half)

        def widened(layer):
            blocks = h_mask.shape[1]
            at_block = layer * (blocks // 2) + lax.broadcasted_iota(jnp.int32, (blocks, cols), 1) // BLOCK
            pick = lax.broadcasted_iota(jnp.int32, (blocks, cols), 0) == at_block
            return jnp.dot(
                h_mask[...].astype(jnp.float32), pick.astype(jnp.float32),
                preferred_element_type=jnp.float32,
            )

        def straight(j):
            push(ham_from(l, j), held(r, l, j), h_sem.at[r, l, j], far)

        def relay(row, layer, j):
            arrived(held(row, layer, j), h_sem.at[row, layer, j])
            push(held(row, layer, j), held(row, layer, j), h_sem.at[row, layer, j], far)

        def relay_end(j):
            relay(end_row, l, j)
            relay(end_row, other, j)

        def split_ham(first, count, j):
            def part(i, _):
                i = first + i
                kept_blocks = masks[i // 2, i % 2, :, chunk(j)]
                for k in range(depth // BLOCK):
                    at_rows = pl.ds(pl.multiple_of(i * depth + k * BLOCK, BLOCK), BLOCK)
                    high, low = split(hbuf[at_rows, chunk(j)] * kept_blocks[k : k + 1, :])
                    hhi[at_rows, chunk(j)] = high
                    hlo[at_rows, chunk(j)] = low
                return 0

            lax.fori_loop(0, count, part, 0)

        def rows_of(half, target, first, count, j, add):
            at_depth = pl.ds(pl.multiple_of(first * depth, depth), count * depth)

            def tile(i, _):
                at_rows = pl.ds(pl.multiple_of(half * rows + i * 256, 256), 256)
                to_rows = pl.ds(pl.multiple_of(i * 256, 256), 256)
                high, h_high = dhi[at_rows, at_depth], hhi[at_depth, chunk(j)]
                total = jnp.dot(high, h_high, preferred_element_type=jnp.float32)
                total += jnp.dot(high, hlo[at_depth, chunk(j)], preferred_element_type=jnp.float32)
                total += jnp.dot(dlo[at_rows, at_depth], h_high, preferred_element_type=jnp.float32)
                if add:
                    total += target[to_rows, chunk(j)]
                target[to_rows, chunk(j)] = total
                return 0

            lax.fori_loop(0, rows // 256, tile, 0)

        near, near_count = (r - 1) * 2, 6
        late, late_count = far_end * 2, 2
        results = []

        def near_end(j):
            for layer in range(2):
                arrived(held(far_row, layer, j), h_sem.at[far_row, layer, j])
            split_ham(near, near_count, j)
            rows_of(1, ends, near, near_count, j, False)

        def late_end(j):
            for layer in range(2):
                arrived(held(far_end, layer, j), h_sem.at[far_end, layer, j])
            split_ham(late, late_count, j)
            rows_of(1, ends, late, late_count, j, True)
            copy = pltpu.make_async_remote_copy(
                src_ref=ends.at[:, chunk(j)], dst_ref=ends.at[:, chunk(j)],
                send_sem=res_send.at[j], recv_sem=res_sem.at[j],
                device_id=end, device_id_type=pl.DeviceIdType.MESH,
            )
            copy.start()
            results.append(copy)

        def near_own(j):
            rows_of(0, out_ref, near, near_count, j, False)

        def late_own(j):
            rows_of(0, out_ref, late, late_count, j, True)

        straight(0)
        mask_dens(0)
        for where in (y, x, s):
            push(piece(own, 0), piece(own, 0), d_sem.at[own, 0], where)
        straight(1)
        for j in range(len(spans)):
            push(ham_from(other, j), held(r, l, j), h_sem.at[r, l, j], y)
        local_h = pltpu.make_async_copy(
            h_ref.at[:, pl.ds(pl.multiple_of(l * cols, cols), cols)],
            hbuf.at[ham_rows(r, l), :], local_sem.at[1],
        )
        local_h.start()
        wide, wide_other = widened(l), widened(other)
        for p in range(masks.shape[0]):
            blocks = slice(p * masks.shape[2], (p + 1) * masks.shape[2])
            masks[p, l] = wide[blocks]
            yours_mask[p] = wide_other[blocks]
        push(yours_mask, masks.at[:, l], mask_sem, y)
        absorb(own, 0)
        take(own, 1, x, s)
        relay(r, other, 0)
        relay(r, other, 1)
        straight(2)
        take(yours, 1, x, s)
        relay(r, other, 2)
        take(yours, 0, x, s)
        relay_end(0)
        take(across * 2 + l, 1, s)
        straight(3)
        relay_end(1)
        take(across * 2 + other, 1, s)
        relay(r, other, 3)
        away = (sibling + 2) % 4
        beside = [col * 2 + layer for col in (sibling, away) for layer in (l, other)]
        for slot in beside:
            take(slot, 1)
        local_h.wait()
        arrived(masks.at[:, other], mask_sem)
        near_end(0)
        late_end(0)
        take(across * 2 + l, 0, s)
        take(across * 2 + other, 0, s)
        near_end(1)
        late_end(1)
        relay_end(2)
        for slot in beside:
            take(slot, 0)
        near_own(0)
        late_own(0)
        near_end(2)
        relay_end(3)
        straight(4)
        relay(r, other, 4)
        near_own(1)
        late_own(1)
        relay_end(4)
        near_own(2)
        late_end(2)
        late_own(2)
        near_end(3)
        near_own(3)
        late_end(3)
        near_end(4)
        near_own(4)
        late_end(4)
        late_own(3)
        late_own(4)
        for copy in sent + results:
            copy.wait_send()


def chunk_spans(cols):
    quarter = cols // 4
    widths = [quarter] * 3 + [quarter // 2] * 2
    return [(sum(widths[:j]), width) for j, width in enumerate(widths)]


def product_of(dens, dens_wide, ham, ham_mask, layers, grid_cols):
    rows, width = dens.shape
    depth, ham_cols = ham.shape
    cols = ham_cols // layers
    inner = layers * grid_cols * width
    planes = inner // (layers * depth)
    chunks = len(chunk_spans(cols))
    f32, bf16 = jnp.float32, jnp.bfloat16
    dma = pltpu.SemaphoreType.DMA
    return pl.pallas_call(
        kernel,
        out_shape=jax.ShapeDtypeStruct((rows, cols), f32),
        in_specs=[
            pl.BlockSpec(memory_space=pltpu.HBM),
            pl.BlockSpec(memory_space=pltpu.VMEM),
            pl.BlockSpec(memory_space=pltpu.HBM),
            pl.BlockSpec(memory_space=pltpu.VMEM),
        ],
        out_specs=pl.BlockSpec(memory_space=pltpu.VMEM),
        scratch_shapes=[
            pltpu.VMEM((layers * grid_cols, 2 * rows, width), f32),
            pltpu.VMEM((inner, cols), f32),
            pltpu.VMEM((rows, width), f32),
            pltpu.VMEM((planes, layers, depth // BLOCK, cols), f32),
            pltpu.VMEM((planes, depth // BLOCK, cols), f32),
            pltpu.VMEM((2 * rows, inner), bf16),
            pltpu.VMEM((2 * rows, inner), bf16),
            pltpu.VMEM((inner, cols), bf16),
            pltpu.VMEM((inner, cols), bf16),
            pltpu.VMEM((rows, cols), f32),
            dma((layers * grid_cols, 2)),
            dma((4, 2, chunks)),
            dma((chunks,)),
            dma((16 + 5 * chunks,)),
            dma((chunks,)),
            dma((2,)),
            dma,
        ],
        compiler_params=pltpu.CompilerParams(
            collective_id=0, has_side_effects=True, vmem_limit_bytes=56 * 2**20
        ),
    )(dens, dens_wide, ham, ham_mask)


def lined_up(density, dens_mask, hamiltonian, ham_mask, filter_mask, *, layers, grid_cols):
    dens_wide = jnp.repeat(dens_mask[0].astype(jnp.float32), BLOCK, axis=1)
    total = product_of(density[0], dens_wide, hamiltonian[0], ham_mask[0], layers, grid_cols)
    kept_blocks = filter_mask.shape[1] // layers
    kept = lax.dynamic_slice_in_dim(filter_mask, lax.axis_index("layer") * kept_blocks, kept_blocks, 1)
    wide = jnp.repeat(kept.astype(jnp.float32), BLOCK, axis=1)
    out = total.reshape(-1, BLOCK, total.shape[1]) * wide[:, None, :]
    return out.reshape(total.shape)


def gathered(density, dens_mask, hamiltonian, ham_mask, filter_mask):
    dens = lax.all_gather(density * expand(dens_mask), "col", axis=2, tiled=True)[0]
    ham = lax.all_gather(masked_ham(hamiltonian, ham_mask), "row", axis=0, tiled=True)
    part = jnp.dot(dens, ham, precision=lax.Precision.HIGHEST, preferred_element_type=jnp.float32)
    return lax.psum_scatter(part * expand(filter_mask), "layer", scatter_dimension=1, tiled=True)


def solution(mesh):
    sizes = dict(mesh.shape)
    layers, grid_cols = sizes["layer"], sizes["col"]
    body = gathered
    if sizes == {"row": 4, "col": 4, "layer": 2}:
        body = functools.partial(lined_up, layers=layers, grid_cols=grid_cols)
    return jax.shard_map(
        body,
        mesh=mesh,
        in_specs=(
            P("layer", "row", "col"),
            P("layer", "row", "col"),
            P("layer", "row", "col"),
            P("layer", None, "col"),
            P("row", "col"),
        ),
        out_specs=P("row", ("col", "layer")),
        check_vma=False,
    )
```

```python
import functools

import jax
import jax.numpy as jnp
from jax import lax
from jax.experimental import pallas as pl
from jax.experimental.pallas import tpu as pltpu
from jax.sharding import PartitionSpec as P

BLOCK = 64


def expand(block_mask):
    widened = jnp.repeat(block_mask.astype(jnp.float32), BLOCK, axis=-2)
    return jnp.repeat(widened, BLOCK, axis=-1)


def masked_ham(hamiltonian, ham_mask):
    blocks = hamiltonian.shape[1] // BLOCK
    mine = lax.dynamic_slice_in_dim(ham_mask[0], lax.axis_index("row") * blocks, blocks, 0)
    wide = jnp.repeat(mine.astype(jnp.float32), BLOCK, axis=1)
    ham = hamiltonian[0].reshape(blocks, BLOCK, -1) * wide[:, None, :]
    return ham.reshape(hamiltonian.shape[1:])


def split(x):
    high = x.astype(jnp.bfloat16)
    return high, (x - high.astype(jnp.float32)).astype(jnp.bfloat16)


def kernel(
    d_ref, d_mask, h_ref, h_mask, f_mask, out_ref,
    dbuf, hbuf, raw, masks, yours_mask, kept, dhi, dlo, hhi, hlo, ends,
    d_sem, h_sem, res_sem, send_sem, res_send, local_sem, mask_sem,
):
    r, c, l = lax.axis_index("row"), lax.axis_index("col"), lax.axis_index("layer")
    rows, width = d_ref.shape
    depth = h_ref.shape[0]
    cols = out_ref.shape[1]
    spans = chunk_spans(cols)
    across = (c + 2) % 4
    sibling = c + 1 - 2 * (c % 2)
    other = 1 - l
    own, yours = c * 2 + l, c * 2 + other
    is_hub = jnp.logical_and(r > 0, r < 3)

    def at(row, col, layer):
        return {"row": row, "col": col, "layer": layer}

    def arrived(ref, recv):
        pltpu.make_async_remote_copy(
            src_ref=ref, dst_ref=ref, send_sem=send_sem.at[0], recv_sem=recv,
            device_id=at(r, c, other), device_id_type=pl.DeviceIdType.MESH,
        ).wait_recv()

    def ham_rows(row, layer):
        return pl.ds(pl.multiple_of((row * 2 + layer) * depth, depth), depth)

    def chunk(j):
        return pl.ds(*spans[j])

    def piece(slot, half):
        return dbuf.at[slot, pl.ds(half * rows, rows), :]

    def ham_from(layer, j):
        first, wide = spans[j]
        return h_ref.at[:, pl.ds(pl.multiple_of(layer * cols + first, 128), wide)]

    def held(row, layer, j):
        return hbuf.at[ham_rows(row, layer), chunk(j)]

    sent = []

    def push(src, dst, recv, where):
        copy = pltpu.make_async_remote_copy(
            src_ref=src, dst_ref=dst, send_sem=send_sem.at[len(sent)], recv_sem=recv,
            device_id=where, device_id_type=pl.DeviceIdType.MESH,
        )
        copy.start()
        sent.append(copy)

    barrier = pltpu.get_barrier_semaphore()

    def greet(partners):
        for where in partners:
            pl.semaphore_signal(barrier, inc=1, device_id=where, device_id_type=pl.DeviceIdType.MESH)
        pl.semaphore_wait(barrier, len(partners))

    def mask_dens(half):
        load.wait()
        block_of = lax.broadcasted_iota(jnp.int32, (1, width), 1) // BLOCK
        for i in range(rows // BLOCK):
            wide = jnp.zeros((1, width), jnp.float32)
            for k in range(width // BLOCK):
                wide = jnp.where(block_of == k, d_mask[k : k + 1, i : i + 1].astype(jnp.float32), wide)
            block = pl.ds(half * rows + i * BLOCK, BLOCK)
            dbuf[own, block, :] = raw[pl.ds(i * BLOCK, BLOCK), :] * wide

    def widened(mask, layer):
        blocks = mask.shape[1]
        at_block = layer * (blocks // 2) + lax.broadcasted_iota(jnp.int32, (blocks, cols), 1) // BLOCK
        pick = lax.broadcasted_iota(jnp.int32, (blocks, cols), 0) == at_block
        return jnp.dot(
            mask[...].astype(jnp.float32), pick.astype(jnp.float32),
            preferred_element_type=jnp.float32,
        )

    def filtered(source, j):
        for i in range(rows // BLOCK):
            block = pl.ds(i * BLOCK, BLOCK)
            out_ref[block, chunk(j)] = source[block, chunk(j)] * kept[pl.ds(i, 1), chunk(j)]

    y = at(r, c, other)
    load = pltpu.make_async_copy(d_ref, raw, local_sem.at[0])
    load.start()

    @pl.when(jnp.logical_not(is_hub))
    def _():
        sent.clear()
        hub = at(1 + r // 3, c, l)
        greet([hub, y])
        push(ham_from(other, 0), held(r, l, 0), h_sem.at[r, l, 0], y)
        mask_dens(1)
        push(piece(own, 1), piece(own, 1), d_sem.at[own, 1], hub)
        push(piece(own, 1), piece(own, 1), d_sem.at[own, 1], y)
        for j in range(1, len(spans)):
            push(ham_from(other, j), held(r, l, j), h_sem.at[r, l, j], y)
        arrived(piece(yours, 1), d_sem.at[yours, 1])
        push(piece(yours, 1), piece(yours, 1), d_sem.at[yours, 1], hub)
        sent[1].wait_send()
        last = len(sent) - 1
        for j in range(len(spans)):
            push(ham_from(l, j), held(r, l, j), h_sem.at[r, l, j], hub)
            arrived(held(r, other, j), h_sem.at[r, other, j])
            push(held(r, other, j), held(r, other, j), h_sem.at[r, other, j], hub)
            if j == 0:
                sent[last].wait_send()
            else:
                sent[last + 2 * j - 1].wait_send()
                sent[last + 2 * j].wait_send()
        waited = {1} | set(range(last, len(sent) - 2))
        kept[...] = widened(f_mask, l)
        for j in range(len(spans)):
            arrived(ends.at[:, chunk(j)], res_sem.at[j])
            filtered(ends, j)
        for i, copy in enumerate(sent):
            if i not in waited:
                copy.wait_send()

    @pl.when(is_hub)
    def _():
        sent.clear()
        end_row, far_row = 3 * r - 3, 3 - r
        far_end = 3 - end_row
        x, s = at(r, across, l), at(r, sibling, l)
        end, far = at(end_row, c, l), at(far_row, c, l)
        greet([y, x, s, end, far])

        def absorb(slot, half):
            def tile(i, _):
                at_rows = pl.ds(pl.multiple_of(half * rows + i * 128, 128), 128)
                high, low = split(dbuf[slot, at_rows, :])
                at_cols = pl.ds(pl.multiple_of(slot * width, width), width)
                dhi[at_rows, at_cols] = high
                dlo[at_rows, at_cols] = low
                return 0

            lax.fori_loop(0, rows // 128, tile, 0)

        def take(slot, half, *partners):
            arrived(piece(slot, half), d_sem.at[slot, half])
            for where in partners:
                push(piece(slot, half), piece(slot, half), d_sem.at[slot, half], where)
            absorb(slot, half)

        def straight(j):
            push(ham_from(l, j), held(r, l, j), h_sem.at[r, l, j], far)

        def relay(row, layer, j):
            arrived(held(row, layer, j), h_sem.at[row, layer, j])
            push(held(row, layer, j), held(row, layer, j), h_sem.at[row, layer, j], far)

        def relay_end(j):
            relay(end_row, l, j)
            relay(end_row, other, j)

        def split_ham(first, count, j):
            def part(i, _):
                i = first + i
                kept_blocks = masks[i // 2, i % 2, :, chunk(j)]
                for k in range(depth // BLOCK):
                    at_rows = pl.ds(pl.multiple_of(i * depth + k * BLOCK, BLOCK), BLOCK)
                    high, low = split(hbuf[at_rows, chunk(j)] * kept_blocks[k : k + 1, :])
                    hhi[at_rows, chunk(j)] = high
                    hlo[at_rows, chunk(j)] = low
                return 0

            lax.fori_loop(0, count, part, 0)

        def rows_of(half, target, first, count, j, add):
            at_depth = pl.ds(pl.multiple_of(first * depth, depth), count * depth)

            def tile(i, _):
                at_rows = pl.ds(pl.multiple_of(half * rows + i * 256, 256), 256)
                to_rows = pl.ds(pl.multiple_of(i * 256, 256), 256)
                high, h_high = dhi[at_rows, at_depth], hhi[at_depth, chunk(j)]
                total = jnp.dot(high, h_high, preferred_element_type=jnp.float32)
                total += jnp.dot(high, hlo[at_depth, chunk(j)], preferred_element_type=jnp.float32)
                total += jnp.dot(dlo[at_rows, at_depth], h_high, preferred_element_type=jnp.float32)
                if add:
                    total += target[to_rows, chunk(j)]
                target[to_rows, chunk(j)] = total
                return 0

            lax.fori_loop(0, rows // 256, tile, 0)

        near, near_count = (r - 1) * 2, 6
        late, late_count = far_end * 2, 2
        results = []

        def near_end(j):
            for layer in range(2):
                arrived(held(far_row, layer, j), h_sem.at[far_row, layer, j])
            split_ham(near, near_count, j)
            rows_of(1, ends, near, near_count, j, False)

        def late_end(j):
            for layer in range(2):
                arrived(held(far_end, layer, j), h_sem.at[far_end, layer, j])
            split_ham(late, late_count, j)
            rows_of(1, ends, late, late_count, j, True)
            copy = pltpu.make_async_remote_copy(
                src_ref=ends.at[:, chunk(j)], dst_ref=ends.at[:, chunk(j)],
                send_sem=res_send.at[j], recv_sem=res_sem.at[j],
                device_id=end, device_id_type=pl.DeviceIdType.MESH,
            )
            copy.start()
            results.append(copy)

        def near_own(j):
            rows_of(0, out_ref, near, near_count, j, False)

        def late_own(j):
            rows_of(0, out_ref, late, late_count, j, True)
            filtered(out_ref, j)

        straight(0)
        mask_dens(0)
        for where in (y, x, s):
            push(piece(own, 0), piece(own, 0), d_sem.at[own, 0], where)
        straight(1)
        for j in range(len(spans)):
            push(ham_from(other, j), held(r, l, j), h_sem.at[r, l, j], y)
        local_h = pltpu.make_async_copy(
            h_ref.at[:, pl.ds(pl.multiple_of(l * cols, cols), cols)],
            hbuf.at[ham_rows(r, l), :], local_sem.at[1],
        )
        local_h.start()
        wide, wide_other = widened(h_mask, l), widened(h_mask, other)
        kept[...] = widened(f_mask, l)
        for p in range(masks.shape[0]):
            blocks = slice(p * masks.shape[2], (p + 1) * masks.shape[2])
            masks[p, l] = wide[blocks]
            yours_mask[p] = wide_other[blocks]
        push(yours_mask, masks.at[:, l], mask_sem, y)
        absorb(own, 0)
        take(own, 1, x, s)
        relay(r, other, 0)
        relay(r, other, 1)
        straight(2)
        take(yours, 1, x, s)
        relay(r, other, 2)
        take(yours, 0, x, s)
        relay_end(0)
        take(across * 2 + l, 1, s)
        straight(3)
        relay_end(1)
        take(across * 2 + other, 1, s)
        relay(r, other, 3)
        away = (sibling + 2) % 4
        beside = [col * 2 + layer for col in (sibling, away) for layer in (l, other)]
        for slot in beside:
            take(slot, 1)
        local_h.wait()
        arrived(masks.at[:, other], mask_sem)
        near_end(0)
        late_end(0)
        take(across * 2 + l, 0, s)
        take(across * 2 + other, 0, s)
        relay_end(2)
        near_end(1)
        for slot in beside:
            take(slot, 0)
        relay_end(3)
        straight(4)
        relay(r, other, 4)
        late_end(1)
        relay_end(4)
        near_end(2)
        near_own(0)
        late_own(0)
        near_own(1)
        late_own(1)
        late_end(2)
        near_own(2)
        late_own(2)
        near_end(3)
        near_own(3)
        late_end(3)
        near_end(4)
        near_own(4)
        late_end(4)
        late_own(3)
        late_own(4)
        for copy in sent + results:
            copy.wait_send()


def chunk_spans(cols):
    quarter = cols // 4
    widths = [quarter] * 3 + [quarter // 2] * 2
    return [(sum(widths[:j]), width) for j, width in enumerate(widths)]


def product_of(dens, dens_mask, ham, ham_mask, filter_mask, layers, grid_cols):
    rows, width = dens.shape
    depth, ham_cols = ham.shape
    cols = ham_cols // layers
    inner = layers * grid_cols * width
    planes = inner // (layers * depth)
    chunks = len(chunk_spans(cols))
    f32, bf16 = jnp.float32, jnp.bfloat16
    dma = pltpu.SemaphoreType.DMA
    return pl.pallas_call(
        kernel,
        out_shape=jax.ShapeDtypeStruct((rows, cols), f32),
        in_specs=[
            pl.BlockSpec(memory_space=pltpu.HBM),
            pl.BlockSpec(memory_space=pltpu.VMEM),
            pl.BlockSpec(memory_space=pltpu.HBM),
            pl.BlockSpec(memory_space=pltpu.VMEM),
            pl.BlockSpec(memory_space=pltpu.VMEM),
        ],
        out_specs=pl.BlockSpec(memory_space=pltpu.VMEM),
        scratch_shapes=[
            pltpu.VMEM((layers * grid_cols, 2 * rows, width), f32),
            pltpu.VMEM((inner, cols), f32),
            pltpu.VMEM((rows, width), f32),
            pltpu.VMEM((planes, layers, depth // BLOCK, cols), f32),
            pltpu.VMEM((planes, depth // BLOCK, cols), f32),
            pltpu.VMEM((rows // BLOCK, cols), f32),
            pltpu.VMEM((2 * rows, inner), bf16),
            pltpu.VMEM((2 * rows, inner), bf16),
            pltpu.VMEM((inner, cols), bf16),
            pltpu.VMEM((inner, cols), bf16),
            pltpu.VMEM((rows, cols), f32),
            dma((layers * grid_cols, 2)),
            dma((4, 2, chunks)),
            dma((chunks,)),
            dma((16 + 5 * chunks,)),
            dma((chunks,)),
            dma((2,)),
            dma,
        ],
        compiler_params=pltpu.CompilerParams(
            collective_id=0, has_side_effects=True, vmem_limit_bytes=50 * 2**20
        ),
    )(dens, dens_mask, ham, ham_mask, filter_mask)


def lined_up(density, dens_mask, hamiltonian, ham_mask, filter_mask, *, layers, grid_cols):
    return product_of(
        density[0], dens_mask[0].T, hamiltonian[0], ham_mask[0], filter_mask, layers, grid_cols
    )


def gathered(density, dens_mask, hamiltonian, ham_mask, filter_mask):
    dens = lax.all_gather(density * expand(dens_mask), "col", axis=2, tiled=True)[0]
    ham = lax.all_gather(masked_ham(hamiltonian, ham_mask), "row", axis=0, tiled=True)
    part = jnp.dot(dens, ham, precision=lax.Precision.HIGHEST, preferred_element_type=jnp.float32)
    return lax.psum_scatter(part * expand(filter_mask), "layer", scatter_dimension=1, tiled=True)


def solution(mesh):
    sizes = dict(mesh.shape)
    layers, grid_cols = sizes["layer"], sizes["col"]
    body = gathered
    if sizes == {"row": 4, "col": 4, "layer": 2}:
        body = functools.partial(lined_up, layers=layers, grid_cols=grid_cols)
    return jax.shard_map(
        body,
        mesh=mesh,
        in_specs=(
            P("layer", "row", "col"),
            P("layer", "row", "col"),
            P("layer", "row", "col"),
            P("layer", None, "col"),
            P("row", "col"),
        ),
        out_specs=P("row", ("col", "layer")),
        check_vma=False,
    )
```

```python
import functools

import jax
import jax.numpy as jnp
from jax import lax
from jax.experimental import pallas as pl
from jax.experimental.pallas import tpu as pltpu
from jax.sharding import PartitionSpec as P

BLOCK = 64


def expand(block_mask):
    widened = jnp.repeat(block_mask.astype(jnp.float32), BLOCK, axis=-2)
    return jnp.repeat(widened, BLOCK, axis=-1)


def masked_ham(hamiltonian, ham_mask):
    blocks = hamiltonian.shape[1] // BLOCK
    mine = lax.dynamic_slice_in_dim(ham_mask[0], lax.axis_index("row") * blocks, blocks, 0)
    wide = jnp.repeat(mine.astype(jnp.float32), BLOCK, axis=1)
    ham = hamiltonian[0].reshape(blocks, BLOCK, -1) * wide[:, None, :]
    return ham.reshape(hamiltonian.shape[1:])


def split(x):
    high = x.astype(jnp.bfloat16)
    return high, (x - high.astype(jnp.float32)).astype(jnp.bfloat16)


def kernel(
    d_ref, d_mask, h_ref, h_mask, f_mask, out_ref,
    dbuf, hbuf, raw, masks, yours_mask, kept, dhi, dlo, hhi, hlo, ends,
    d_sem, h_sem, res_sem, send_sem, res_send, local_sem, mask_sem,
):
    r, c, l = lax.axis_index("row"), lax.axis_index("col"), lax.axis_index("layer")
    rows, width = d_ref.shape
    depth = h_ref.shape[0]
    cols = out_ref.shape[1]
    spans = chunk_spans(cols)
    across = (c + 2) % 4
    sibling = c + 1 - 2 * (c % 2)
    other = 1 - l
    own, yours = c * 2 + l, c * 2 + other
    is_hub = jnp.logical_and(r > 0, r < 3)

    def at(row, col, layer):
        return {"row": row, "col": col, "layer": layer}

    def arrived(ref, recv):
        pltpu.make_async_remote_copy(
            src_ref=ref, dst_ref=ref, send_sem=send_sem.at[0], recv_sem=recv,
            device_id=at(r, c, other), device_id_type=pl.DeviceIdType.MESH,
        ).wait_recv()

    def ham_rows(row, layer):
        return pl.ds(pl.multiple_of((row * 2 + layer) * depth, depth), depth)

    def chunk(j):
        return pl.ds(*spans[j])

    def piece(slot, half):
        return dbuf.at[slot, pl.ds(half * rows, rows), :]

    def ham_from(layer, j):
        first, wide = spans[j]
        return h_ref.at[:, pl.ds(pl.multiple_of(layer * cols + first, 128), wide)]

    def held(row, layer, j):
        return hbuf.at[ham_rows(row, layer), chunk(j)]

    sent = []

    def push(src, dst, recv, where):
        copy = pltpu.make_async_remote_copy(
            src_ref=src, dst_ref=dst, send_sem=send_sem.at[len(sent)], recv_sem=recv,
            device_id=where, device_id_type=pl.DeviceIdType.MESH,
        )
        copy.start()
        sent.append(copy)

    barrier = pltpu.get_barrier_semaphore()

    def greet(partners):
        for where in partners:
            pl.semaphore_signal(barrier, inc=1, device_id=where, device_id_type=pl.DeviceIdType.MESH)
        pl.semaphore_wait(barrier, len(partners))

    def mask_dens(half):
        load.wait()
        block_of = lax.broadcasted_iota(jnp.int32, (1, width), 1) // BLOCK
        for i in range(rows // BLOCK):
            wide = jnp.zeros((1, width), jnp.float32)
            for k in range(width // BLOCK):
                wide = jnp.where(block_of == k, d_mask[k : k + 1, i : i + 1].astype(jnp.float32), wide)
            block = pl.ds(half * rows + i * BLOCK, BLOCK)
            dbuf[own, block, :] = raw[pl.ds(i * BLOCK, BLOCK), :] * wide

    def widened(mask, layer):
        blocks = mask.shape[1]
        at_block = layer * (blocks // 2) + lax.broadcasted_iota(jnp.int32, (blocks, cols), 1) // BLOCK
        pick = lax.broadcasted_iota(jnp.int32, (blocks, cols), 0) == at_block
        return jnp.dot(
            mask[...].astype(jnp.float32), pick.astype(jnp.float32),
            preferred_element_type=jnp.float32,
        )

    def filtered(source, j):
        for i in range(rows // BLOCK):
            block = pl.ds(i * BLOCK, BLOCK)
            out_ref[block, chunk(j)] = source[block, chunk(j)] * kept[pl.ds(i, 1), chunk(j)]

    y = at(r, c, other)
    load = pltpu.make_async_copy(d_ref, raw, local_sem.at[0])
    load.start()

    @pl.when(jnp.logical_not(is_hub))
    def _():
        sent.clear()
        hub = at(1 + r // 3, c, l)
        greet([hub, y])
        mask_dens(1)
        push(piece(own, 1), piece(own, 1), d_sem.at[own, 1], y)
        push(piece(own, 1), piece(own, 1), d_sem.at[own, 1], hub)
        for j in range(len(spans)):
            push(ham_from(other, j), held(r, l, j), h_sem.at[r, l, j], y)
            if j == 0:
                sent[0].wait_send()
        arrived(piece(yours, 1), d_sem.at[yours, 1])
        push(piece(yours, 1), piece(yours, 1), d_sem.at[yours, 1], hub)
        last = len(sent) - 1
        sent[1].wait_send()
        sent[last].wait_send()
        for j in range(len(spans)):
            push(ham_from(l, j), held(r, l, j), h_sem.at[r, l, j], hub)
            arrived(held(r, other, j), h_sem.at[r, other, j])
            push(held(r, other, j), held(r, other, j), h_sem.at[r, other, j], hub)
            if j > 0:
                sent[last + 2 * j - 1].wait_send()
                sent[last + 2 * j].wait_send()
        waited = {0, 1} | set(range(last, len(sent) - 2))
        kept[...] = widened(f_mask, l)
        for j in range(len(spans)):
            arrived(ends.at[:, chunk(j)], res_sem.at[j])
            filtered(ends, j)
        for i, copy in enumerate(sent):
            if i not in waited:
                copy.wait_send()

    @pl.when(is_hub)
    def _():
        sent.clear()
        end_row, far_row = 3 * r - 3, 3 - r
        far_end = 3 - end_row
        x, s = at(r, across, l), at(r, sibling, l)
        end, far = at(end_row, c, l), at(far_row, c, l)
        greet([y, x, s, end, far])

        def absorb(slot, half):
            def tile(i, _):
                at_rows = pl.ds(pl.multiple_of(half * rows + i * 128, 128), 128)
                high, low = split(dbuf[slot, at_rows, :])
                at_cols = pl.ds(pl.multiple_of(slot * width, width), width)
                dhi[at_rows, at_cols] = high
                dlo[at_rows, at_cols] = low
                return 0

            lax.fori_loop(0, rows // 128, tile, 0)

        def take(slot, half, *partners):
            arrived(piece(slot, half), d_sem.at[slot, half])
            for where in partners:
                push(piece(slot, half), piece(slot, half), d_sem.at[slot, half], where)
            absorb(slot, half)

        def straight(j):
            push(ham_from(l, j), held(r, l, j), h_sem.at[r, l, j], far)

        def relay(row, layer, j):
            arrived(held(row, layer, j), h_sem.at[row, layer, j])
            push(held(row, layer, j), held(row, layer, j), h_sem.at[row, layer, j], far)

        def relay_end(j):
            relay(end_row, l, j)
            relay(end_row, other, j)

        def split_ham(first, count, j):
            def part(i, _):
                i = first + i
                kept_blocks = masks[i // 2, i % 2, :, chunk(j)]
                for k in range(depth // BLOCK):
                    at_rows = pl.ds(pl.multiple_of(i * depth + k * BLOCK, BLOCK), BLOCK)
                    high, low = split(hbuf[at_rows, chunk(j)] * kept_blocks[k : k + 1, :])
                    hhi[at_rows, chunk(j)] = high
                    hlo[at_rows, chunk(j)] = low
                return 0

            lax.fori_loop(0, count, part, 0)

        def rows_of(half, target, first, count, j, add):
            at_depth = pl.ds(pl.multiple_of(first * depth, depth), count * depth)

            def tile(i, _):
                at_rows = pl.ds(pl.multiple_of(half * rows + i * 256, 256), 256)
                to_rows = pl.ds(pl.multiple_of(i * 256, 256), 256)
                high, h_high = dhi[at_rows, at_depth], hhi[at_depth, chunk(j)]
                total = jnp.dot(high, h_high, preferred_element_type=jnp.float32)
                total += jnp.dot(high, hlo[at_depth, chunk(j)], preferred_element_type=jnp.float32)
                total += jnp.dot(dlo[at_rows, at_depth], h_high, preferred_element_type=jnp.float32)
                if add:
                    total += target[to_rows, chunk(j)]
                target[to_rows, chunk(j)] = total
                return 0

            lax.fori_loop(0, rows // 256, tile, 0)

        near, near_count = (r - 1) * 2, 6
        late, late_count = far_end * 2, 2
        results = []

        def near_end(j):
            for layer in range(2):
                arrived(held(far_row, layer, j), h_sem.at[far_row, layer, j])
            split_ham(near, near_count, j)
            rows_of(1, ends, near, near_count, j, False)

        def late_end(j):
            for layer in range(2):
                arrived(held(far_end, layer, j), h_sem.at[far_end, layer, j])
            split_ham(late, late_count, j)
            rows_of(1, ends, late, late_count, j, True)
            copy = pltpu.make_async_remote_copy(
                src_ref=ends.at[:, chunk(j)], dst_ref=ends.at[:, chunk(j)],
                send_sem=res_send.at[j], recv_sem=res_sem.at[j],
                device_id=end, device_id_type=pl.DeviceIdType.MESH,
            )
            copy.start()
            results.append(copy)

        def near_own(j):
            rows_of(0, out_ref, near, near_count, j, False)

        def late_own(j):
            rows_of(0, out_ref, late, late_count, j, True)
            filtered(out_ref, j)

        def swap(j):
            push(ham_from(other, j), held(r, l, j), h_sem.at[r, l, j], y)

        straight(0)
        swap(0)
        straight(1)
        swap(1)
        mask_dens(0)
        for where in (x, s):
            push(piece(own, 0), piece(own, 0), d_sem.at[own, 0], where)
        straight(2)
        local_h = pltpu.make_async_copy(
            h_ref.at[:, pl.ds(pl.multiple_of(l * cols, cols), cols)],
            hbuf.at[ham_rows(r, l), :], local_sem.at[1],
        )
        local_h.start()
        wide, wide_other = widened(h_mask, l), widened(h_mask, other)
        kept[...] = widened(f_mask, l)
        for p in range(masks.shape[0]):
            blocks = slice(p * masks.shape[2], (p + 1) * masks.shape[2])
            masks[p, l] = wide[blocks]
            yours_mask[p] = wide_other[blocks]
        push(yours_mask, masks.at[:, l], mask_sem, y)
        absorb(own, 0)
        relay(r, other, 0)
        swap(2)
        relay(r, other, 1)
        swap(3)
        swap(4)
        take(own, 1, x, s)
        relay(r, other, 2)
        take(yours, 1, x, s)
        push(piece(own, 0), piece(own, 0), d_sem.at[own, 0], y)
        relay_end(0)
        take(across * 2 + l, 1, s)
        straight(3)
        relay_end(1)
        take(across * 2 + other, 1, s)
        relay(r, other, 3)
        away = (sibling + 2) % 4
        beside = [col * 2 + layer for col in (sibling, away) for layer in (l, other)]
        for slot in beside:
            take(slot, 1)
        local_h.wait()
        arrived(masks.at[:, other], mask_sem)
        near_end(0)
        take(yours, 0, x, s)
        late_end(0)
        take(across * 2 + l, 0, s)
        relay_end(2)
        take(across * 2 + other, 0, s)
        near_end(1)
        for slot in beside:
            take(slot, 0)
        relay_end(3)
        straight(4)
        relay(r, other, 4)
        late_end(1)
        relay_end(4)
        near_end(2)
        near_own(0)
        late_own(0)
        near_own(1)
        late_own(1)
        late_end(2)
        near_own(2)
        late_own(2)
        near_end(3)
        near_own(3)
        late_end(3)
        near_end(4)
        near_own(4)
        late_end(4)
        late_own(3)
        late_own(4)
        for copy in sent + results:
            copy.wait_send()


def chunk_spans(cols):
    quarter = cols // 4
    widths = [quarter] * 3 + [quarter // 2] * 2
    return [(sum(widths[:j]), width) for j, width in enumerate(widths)]


def product_of(dens, dens_mask, ham, ham_mask, filter_mask, layers, grid_cols):
    rows, width = dens.shape
    depth, ham_cols = ham.shape
    cols = ham_cols // layers
    inner = layers * grid_cols * width
    planes = inner // (layers * depth)
    chunks = len(chunk_spans(cols))
    f32, bf16 = jnp.float32, jnp.bfloat16
    dma = pltpu.SemaphoreType.DMA
    return pl.pallas_call(
        kernel,
        out_shape=jax.ShapeDtypeStruct((rows, cols), f32),
        in_specs=[
            pl.BlockSpec(memory_space=pltpu.HBM),
            pl.BlockSpec(memory_space=pltpu.VMEM),
            pl.BlockSpec(memory_space=pltpu.HBM),
            pl.BlockSpec(memory_space=pltpu.VMEM),
            pl.BlockSpec(memory_space=pltpu.VMEM),
        ],
        out_specs=pl.BlockSpec(memory_space=pltpu.VMEM),
        scratch_shapes=[
            pltpu.VMEM((layers * grid_cols, 2 * rows, width), f32),
            pltpu.VMEM((inner, cols), f32),
            pltpu.VMEM((rows, width), f32),
            pltpu.VMEM((planes, layers, depth // BLOCK, cols), f32),
            pltpu.VMEM((planes, depth // BLOCK, cols), f32),
            pltpu.VMEM((rows // BLOCK, cols), f32),
            pltpu.VMEM((2 * rows, inner), bf16),
            pltpu.VMEM((2 * rows, inner), bf16),
            pltpu.VMEM((inner, cols), bf16),
            pltpu.VMEM((inner, cols), bf16),
            pltpu.VMEM((rows, cols), f32),
            dma((layers * grid_cols, 2)),
            dma((4, 2, chunks)),
            dma((chunks,)),
            dma((16 + 5 * chunks,)),
            dma((chunks,)),
            dma((2,)),
            dma,
        ],
        compiler_params=pltpu.CompilerParams(
            collective_id=0, has_side_effects=True, vmem_limit_bytes=50 * 2**20
        ),
    )(dens, dens_mask, ham, ham_mask, filter_mask)


def lined_up(density, dens_mask, hamiltonian, ham_mask, filter_mask, *, layers, grid_cols):
    return product_of(
        density[0], dens_mask[0].T, hamiltonian[0], ham_mask[0], filter_mask, layers, grid_cols
    )


def gathered(density, dens_mask, hamiltonian, ham_mask, filter_mask):
    dens = lax.all_gather(density * expand(dens_mask), "col", axis=2, tiled=True)[0]
    ham = lax.all_gather(masked_ham(hamiltonian, ham_mask), "row", axis=0, tiled=True)
    part = jnp.dot(dens, ham, precision=lax.Precision.HIGHEST, preferred_element_type=jnp.float32)
    return lax.psum_scatter(part * expand(filter_mask), "layer", scatter_dimension=1, tiled=True)


def solution(mesh):
    sizes = dict(mesh.shape)
    layers, grid_cols = sizes["layer"], sizes["col"]
    body = gathered
    if sizes == {"row": 4, "col": 4, "layer": 2}:
        body = functools.partial(lined_up, layers=layers, grid_cols=grid_cols)
    return jax.shard_map(
        body,
        mesh=mesh,
        in_specs=(
            P("layer", "row", "col"),
            P("layer", "row", "col"),
            P("layer", "row", "col"),
            P("layer", None, "col"),
            P("row", "col"),
        ),
        out_specs=P("row", ("col", "layer")),
        check_vma=False,
    )
```

```python
import functools

import jax
import jax.numpy as jnp
from jax import lax
from jax.experimental import pallas as pl
from jax.experimental.pallas import tpu as pltpu
from jax.sharding import PartitionSpec as P

BLOCK = 64


def expand(block_mask):
    widened = jnp.repeat(block_mask.astype(jnp.float32), BLOCK, axis=-2)
    return jnp.repeat(widened, BLOCK, axis=-1)


def masked_ham(hamiltonian, ham_mask):
    blocks = hamiltonian.shape[1] // BLOCK
    mine = lax.dynamic_slice_in_dim(ham_mask[0], lax.axis_index("row") * blocks, blocks, 0)
    wide = jnp.repeat(mine.astype(jnp.float32), BLOCK, axis=1)
    ham = hamiltonian[0].reshape(blocks, BLOCK, -1) * wide[:, None, :]
    return ham.reshape(hamiltonian.shape[1:])


def split(x):
    high = x.astype(jnp.bfloat16)
    return high, (x - high.astype(jnp.float32)).astype(jnp.bfloat16)


def kernel(
    d_ref, h_ref, packed, out_ref,
    dbuf, hbuf, raw, masks, yours_mask, kept, dhi, dlo, hhi, hlo, ends,
    d_sem, h_sem, res_sem, send_sem, res_send, local_sem, mask_sem,
):
    r, c, l = lax.axis_index("row"), lax.axis_index("col"), lax.axis_index("layer")
    rows, width = d_ref.shape
    cut = rows // BLOCK
    h_mask, f_mask, d_mask = packed.at[2 * cut :], packed.at[:cut], packed.at[cut : 2 * cut]
    depth = h_ref.shape[0]
    cols = out_ref.shape[1]
    spans = chunk_spans(cols)
    across = (c + 2) % 4
    sibling = c + 1 - 2 * (c % 2)
    other = 1 - l
    own, yours = c * 2 + l, c * 2 + other
    is_hub = jnp.logical_and(r > 0, r < 3)

    def at(row, col, layer):
        return {"row": row, "col": col, "layer": layer}

    def arrived(ref, recv):
        pltpu.make_async_remote_copy(
            src_ref=ref, dst_ref=ref, send_sem=send_sem.at[0], recv_sem=recv,
            device_id=at(r, c, other), device_id_type=pl.DeviceIdType.MESH,
        ).wait_recv()

    def ham_rows(row, layer):
        return pl.ds(pl.multiple_of((row * 2 + layer) * depth, depth), depth)

    def chunk(j):
        return pl.ds(*spans[j])

    def piece(slot, half):
        return dbuf.at[slot, pl.ds(half * rows, rows), :]

    def ham_from(layer, j):
        first, wide = spans[j]
        return h_ref.at[:, pl.ds(pl.multiple_of(layer * cols + first, 128), wide)]

    def held(row, layer, j):
        return hbuf.at[ham_rows(row, layer), chunk(j)]

    sent = []

    def push(src, dst, recv, where):
        copy = pltpu.make_async_remote_copy(
            src_ref=src, dst_ref=dst, send_sem=send_sem.at[len(sent)], recv_sem=recv,
            device_id=where, device_id_type=pl.DeviceIdType.MESH,
        )
        copy.start()
        sent.append(copy)

    barrier = pltpu.get_barrier_semaphore()

    def greet(partners):
        for where in partners:
            pl.semaphore_signal(barrier, inc=1, device_id=where, device_id_type=pl.DeviceIdType.MESH)
        pl.semaphore_wait(barrier, len(partners))

    def mask_dens(half):
        load.wait()
        block_of = lax.broadcasted_iota(jnp.int32, (1, width), 1) // BLOCK
        for i in range(rows // BLOCK):
            wide = jnp.zeros((1, width), jnp.float32)
            for k in range(width // BLOCK):
                wide = jnp.where(block_of == k, d_mask[k : k + 1, i : i + 1].astype(jnp.float32), wide)
            block = pl.ds(half * rows + i * BLOCK, BLOCK)
            dbuf[own, block, :] = raw[pl.ds(i * BLOCK, BLOCK), :] * wide

    def widened(mask, layer):
        blocks = mask.shape[1]
        at_block = layer * (blocks // 2) + lax.broadcasted_iota(jnp.int32, (blocks, cols), 1) // BLOCK
        pick = lax.broadcasted_iota(jnp.int32, (blocks, cols), 0) == at_block
        return jnp.dot(
            mask[...].astype(jnp.float32), pick.astype(jnp.float32),
            preferred_element_type=jnp.float32,
        )

    def filtered(source, j):
        for i in range(rows // BLOCK):
            block = pl.ds(i * BLOCK, BLOCK)
            out_ref[block, chunk(j)] = source[block, chunk(j)] * kept[pl.ds(i, 1), chunk(j)]

    y = at(r, c, other)
    load = pltpu.make_async_copy(d_ref, raw, local_sem.at[0])
    load.start()

    @pl.when(jnp.logical_not(is_hub))
    def _():
        sent.clear()
        hub = at(1 + r // 3, c, l)
        greet([hub, y])
        mask_dens(1)
        push(piece(own, 1), piece(own, 1), d_sem.at[own, 1], y)
        push(piece(own, 1), piece(own, 1), d_sem.at[own, 1], hub)
        for j in range(len(spans)):
            push(ham_from(other, j), held(r, l, j), h_sem.at[r, l, j], y)
            if j == 0:
                sent[0].wait_send()
        arrived(piece(yours, 1), d_sem.at[yours, 1])
        push(piece(yours, 1), piece(yours, 1), d_sem.at[yours, 1], hub)
        last = len(sent) - 1
        sent[1].wait_send()
        sent[last].wait_send()
        for j in range(len(spans)):
            push(ham_from(l, j), held(r, l, j), h_sem.at[r, l, j], hub)
            arrived(held(r, other, j), h_sem.at[r, other, j])
            push(held(r, other, j), held(r, other, j), h_sem.at[r, other, j], hub)
            if j > 0:
                sent[last + 2 * j - 1].wait_send()
                sent[last + 2 * j].wait_send()
        waited = {0, 1} | set(range(last, len(sent) - 2))
        kept[...] = widened(f_mask, l)
        for j in range(len(spans)):
            arrived(ends.at[:, chunk(j)], res_sem.at[j])
            filtered(ends, j)
        for i, copy in enumerate(sent):
            if i not in waited:
                copy.wait_send()

    @pl.when(is_hub)
    def _():
        sent.clear()
        end_row, far_row = 3 * r - 3, 3 - r
        far_end = 3 - end_row
        x, s = at(r, across, l), at(r, sibling, l)
        end, far = at(end_row, c, l), at(far_row, c, l)
        greet([y, x, s, end, far])

        def absorb(slot, half):
            def tile(i, _):
                at_rows = pl.ds(pl.multiple_of(half * rows + i * 128, 128), 128)
                high, low = split(dbuf[slot, at_rows, :])
                at_cols = pl.ds(pl.multiple_of(slot * width, width), width)
                dhi[at_rows, at_cols] = high
                dlo[at_rows, at_cols] = low
                return 0

            lax.fori_loop(0, rows // 128, tile, 0)

        def take(slot, half, *partners):
            arrived(piece(slot, half), d_sem.at[slot, half])
            for where in partners:
                push(piece(slot, half), piece(slot, half), d_sem.at[slot, half], where)
            absorb(slot, half)

        def straight(j):
            push(ham_from(l, j), held(r, l, j), h_sem.at[r, l, j], far)

        def relay(row, layer, j):
            arrived(held(row, layer, j), h_sem.at[row, layer, j])
            push(held(row, layer, j), held(row, layer, j), h_sem.at[row, layer, j], far)

        def relay_end(j):
            relay(end_row, l, j)
            relay(end_row, other, j)

        def split_ham(first, count, j):
            def part(i, _):
                i = first + i
                kept_blocks = masks[i // 2, i % 2, :, chunk(j)]
                for k in range(depth // BLOCK):
                    at_rows = pl.ds(pl.multiple_of(i * depth + k * BLOCK, BLOCK), BLOCK)
                    high, low = split(hbuf[at_rows, chunk(j)] * kept_blocks[k : k + 1, :])
                    hhi[at_rows, chunk(j)] = high
                    hlo[at_rows, chunk(j)] = low
                return 0

            lax.fori_loop(0, count, part, 0)

        def rows_of(half, target, first, count, j, add):
            at_depth = pl.ds(pl.multiple_of(first * depth, depth), count * depth)

            def tile(i, _):
                at_rows = pl.ds(pl.multiple_of(half * rows + i * 256, 256), 256)
                to_rows = pl.ds(pl.multiple_of(i * 256, 256), 256)
                high, h_high = dhi[at_rows, at_depth], hhi[at_depth, chunk(j)]
                total = jnp.dot(high, h_high, preferred_element_type=jnp.float32)
                total += jnp.dot(high, hlo[at_depth, chunk(j)], preferred_element_type=jnp.float32)
                total += jnp.dot(dlo[at_rows, at_depth], h_high, preferred_element_type=jnp.float32)
                if add:
                    total += target[to_rows, chunk(j)]
                target[to_rows, chunk(j)] = total
                return 0

            lax.fori_loop(0, rows // 256, tile, 0)

        near, near_count = (r - 1) * 2, 6
        late, late_count = far_end * 2, 2
        results = []

        def near_end(j):
            for layer in range(2):
                arrived(held(far_row, layer, j), h_sem.at[far_row, layer, j])
            split_ham(near, near_count, j)
            rows_of(1, ends, near, near_count, j, False)

        def late_end(j):
            for layer in range(2):
                arrived(held(far_end, layer, j), h_sem.at[far_end, layer, j])
            split_ham(late, late_count, j)
            rows_of(1, ends, late, late_count, j, True)
            copy = pltpu.make_async_remote_copy(
                src_ref=ends.at[:, chunk(j)], dst_ref=ends.at[:, chunk(j)],
                send_sem=res_send.at[j], recv_sem=res_sem.at[j],
                device_id=end, device_id_type=pl.DeviceIdType.MESH,
            )
            copy.start()
            results.append(copy)

        def near_own(j):
            rows_of(0, out_ref, near, near_count, j, False)

        def late_own(j):
            rows_of(0, out_ref, late, late_count, j, True)
            filtered(out_ref, j)

        def swap(j):
            push(ham_from(other, j), held(r, l, j), h_sem.at[r, l, j], y)

        straight(0)
        swap(0)
        straight(1)
        swap(1)
        mask_dens(0)
        for where in (x, s):
            push(piece(own, 0), piece(own, 0), d_sem.at[own, 0], where)
        straight(2)
        local_h = pltpu.make_async_copy(
            h_ref.at[:, pl.ds(pl.multiple_of(l * cols, cols), cols)],
            hbuf.at[ham_rows(r, l), :], local_sem.at[1],
        )
        local_h.start()
        wide, wide_other = widened(h_mask, l), widened(h_mask, other)
        kept[...] = widened(f_mask, l)
        for p in range(masks.shape[0]):
            blocks = slice(p * masks.shape[2], (p + 1) * masks.shape[2])
            masks[p, l] = wide[blocks]
            yours_mask[p] = wide_other[blocks]
        push(yours_mask, masks.at[:, l], mask_sem, y)
        absorb(own, 0)
        relay(r, other, 0)
        swap(2)
        relay(r, other, 1)
        swap(3)
        swap(4)
        take(own, 1, x, s)
        relay(r, other, 2)
        take(yours, 1, x, s)
        push(piece(own, 0), piece(own, 0), d_sem.at[own, 0], y)
        relay_end(0)
        take(across * 2 + l, 1, s)
        straight(3)
        relay_end(1)
        take(across * 2 + other, 1, s)
        relay(r, other, 3)
        away = (sibling + 2) % 4
        beside = [col * 2 + layer for col in (sibling, away) for layer in (l, other)]
        for slot in beside:
            take(slot, 1)
        local_h.wait()
        arrived(masks.at[:, other], mask_sem)
        near_end(0)
        take(yours, 0, x, s)
        late_end(0)
        take(across * 2 + l, 0, s)
        relay_end(2)
        take(across * 2 + other, 0, s)
        near_end(1)
        for slot in beside:
            take(slot, 0)
        relay_end(3)
        straight(4)
        relay(r, other, 4)
        late_end(1)
        relay_end(4)
        near_end(2)
        near_own(0)
        late_own(0)
        near_own(1)
        late_own(1)
        late_end(2)
        near_own(2)
        late_own(2)
        near_end(3)
        near_own(3)
        late_end(3)
        near_end(4)
        near_own(4)
        late_end(4)
        late_own(3)
        late_own(4)
        for copy in sent + results:
            copy.wait_send()


def chunk_spans(cols):
    quarter = cols // 4
    widths = [quarter] * 3 + [quarter // 2] * 2
    return [(sum(widths[:j]), width) for j, width in enumerate(widths)]


def product_of(dens, ham, packed, layers, grid_cols):
    rows, width = dens.shape
    depth, ham_cols = ham.shape
    cols = ham_cols // layers
    inner = layers * grid_cols * width
    planes = inner // (layers * depth)
    chunks = len(chunk_spans(cols))
    f32, bf16 = jnp.float32, jnp.bfloat16
    dma = pltpu.SemaphoreType.DMA
    return pl.pallas_call(
        kernel,
        out_shape=jax.ShapeDtypeStruct((rows, cols), f32),
        in_specs=[
            pl.BlockSpec(memory_space=pltpu.HBM),
            pl.BlockSpec(memory_space=pltpu.HBM),
            pl.BlockSpec(memory_space=pltpu.VMEM),
        ],
        out_specs=pl.BlockSpec(memory_space=pltpu.VMEM),
        scratch_shapes=[
            pltpu.VMEM((layers * grid_cols, 2 * rows, width), f32),
            pltpu.VMEM((inner, cols), f32),
            pltpu.VMEM((rows, width), f32),
            pltpu.VMEM((planes, layers, depth // BLOCK, cols), f32),
            pltpu.VMEM((planes, depth // BLOCK, cols), f32),
            pltpu.VMEM((rows // BLOCK, cols), f32),
            pltpu.VMEM((2 * rows, inner), bf16),
            pltpu.VMEM((2 * rows, inner), bf16),
            pltpu.VMEM((inner, cols), bf16),
            pltpu.VMEM((inner, cols), bf16),
            pltpu.VMEM((rows, cols), f32),
            dma((layers * grid_cols, 2)),
            dma((4, 2, chunks)),
            dma((chunks,)),
            dma((16 + 5 * chunks,)),
            dma((chunks,)),
            dma((2,)),
            dma,
        ],
        compiler_params=pltpu.CompilerParams(
            collective_id=0, has_side_effects=True, vmem_limit_bytes=50 * 2**20
        ),
    )(dens, ham, packed)


def lined_up(density, dens_mask, hamiltonian, ham_mask, filter_mask, *, layers, grid_cols):
    blocks, across = filter_mask.shape
    small = dens_mask[0].T
    small = jnp.pad(small, ((0, blocks - small.shape[0]), (0, across - small.shape[1])))
    packed = jnp.concatenate([filter_mask, small, ham_mask[0]], axis=0)
    return product_of(density[0], hamiltonian[0], packed, layers, grid_cols)


def gathered(density, dens_mask, hamiltonian, ham_mask, filter_mask):
    dens = lax.all_gather(density * expand(dens_mask), "col", axis=2, tiled=True)[0]
    ham = lax.all_gather(masked_ham(hamiltonian, ham_mask), "row", axis=0, tiled=True)
    part = jnp.dot(dens, ham, precision=lax.Precision.HIGHEST, preferred_element_type=jnp.float32)
    return lax.psum_scatter(part * expand(filter_mask), "layer", scatter_dimension=1, tiled=True)


def solution(mesh):
    sizes = dict(mesh.shape)
    layers, grid_cols = sizes["layer"], sizes["col"]
    body = gathered
    if sizes == {"row": 4, "col": 4, "layer": 2}:
        body = functools.partial(lined_up, layers=layers, grid_cols=grid_cols)
    return jax.shard_map(
        body,
        mesh=mesh,
        in_specs=(
            P("layer", "row", "col"),
            P("layer", "row", "col"),
            P("layer", "row", "col"),
            P("layer", None, "col"),
            P("row", "col"),
        ),
        out_specs=P("row", ("col", "layer")),
        check_vma=False,
    )
```

```python
import functools

import jax
import jax.numpy as jnp
from jax import lax
from jax.experimental import pallas as pl
from jax.experimental.pallas import tpu as pltpu
from jax.sharding import PartitionSpec as P

BLOCK = 64


def expand(block_mask):
    widened = jnp.repeat(block_mask.astype(jnp.float32), BLOCK, axis=-2)
    return jnp.repeat(widened, BLOCK, axis=-1)


def masked_ham(hamiltonian, ham_mask):
    blocks = hamiltonian.shape[1] // BLOCK
    mine = lax.dynamic_slice_in_dim(ham_mask[0], lax.axis_index("row") * blocks, blocks, 0)
    wide = jnp.repeat(mine.astype(jnp.float32), BLOCK, axis=1)
    ham = hamiltonian[0].reshape(blocks, BLOCK, -1) * wide[:, None, :]
    return ham.reshape(hamiltonian.shape[1:])


def split(x):
    high = x.astype(jnp.bfloat16)
    return high, (x - high.astype(jnp.float32)).astype(jnp.bfloat16)


def kernel(
    d_ref, h_ref, packed, out_ref,
    dbuf, hbuf, raw, masks, yours_mask, kept, dhi, dlo, hhi, hlo, ends,
    d_sem, h_sem, res_sem, send_sem, res_send, local_sem, mask_sem,
):
    r, c, l = lax.axis_index("row"), lax.axis_index("col"), lax.axis_index("layer")
    rows, width = d_ref.shape
    cut = rows // BLOCK
    h_mask, f_mask, d_mask = packed.at[2 * cut :], packed.at[:cut], packed.at[cut : 2 * cut]
    depth = h_ref.shape[0]
    cols = out_ref.shape[1]
    spans = chunk_spans(cols)
    across = (c + 2) % 4
    sibling = c + 1 - 2 * (c % 2)
    other = 1 - l
    own, yours = c * 2 + l, c * 2 + other
    is_hub = jnp.logical_and(r > 0, r < 3)

    def at(row, col, layer):
        return {"row": row, "col": col, "layer": layer}

    def arrived(ref, recv):
        pltpu.make_async_remote_copy(
            src_ref=ref, dst_ref=ref, send_sem=send_sem.at[0], recv_sem=recv,
            device_id=at(r, c, other), device_id_type=pl.DeviceIdType.MESH,
        ).wait_recv()

    def ham_rows(row, layer):
        return pl.ds(pl.multiple_of((row * 2 + layer) * depth, depth), depth)

    def chunk(j):
        return pl.ds(*spans[j])

    def piece(slot, half):
        return dbuf.at[slot, pl.ds(half * rows, rows), :]

    def ham_from(layer, j):
        first, wide = spans[j]
        return h_ref.at[:, pl.ds(pl.multiple_of(layer * cols + first, 128), wide)]

    def held(row, layer, j):
        return hbuf.at[ham_rows(row, layer), chunk(j)]

    sent = []

    def push(src, dst, recv, where):
        copy = pltpu.make_async_remote_copy(
            src_ref=src, dst_ref=dst, send_sem=send_sem.at[len(sent)], recv_sem=recv,
            device_id=where, device_id_type=pl.DeviceIdType.MESH,
        )
        copy.start()
        sent.append(copy)

    barrier = pltpu.get_barrier_semaphore()

    def greet(partners):
        for where in partners:
            pl.semaphore_signal(barrier, inc=1, device_id=where, device_id_type=pl.DeviceIdType.MESH)
        pl.semaphore_wait(barrier, len(partners))

    def mask_dens(half):
        load.wait()
        block_of = lax.broadcasted_iota(jnp.int32, (1, width), 1) // BLOCK
        for i in range(rows // BLOCK):
            wide = jnp.zeros((1, width), jnp.float32)
            for k in range(width // BLOCK):
                wide = jnp.where(block_of == k, d_mask[k : k + 1, i : i + 1].astype(jnp.float32), wide)
            block = pl.ds(half * rows + i * BLOCK, BLOCK)
            dbuf[own, block, :] = raw[pl.ds(i * BLOCK, BLOCK), :] * wide

    def widened(mask, layer):
        blocks = mask.shape[1]
        at_block = layer * (blocks // 2) + lax.broadcasted_iota(jnp.int32, (blocks, cols), 1) // BLOCK
        pick = lax.broadcasted_iota(jnp.int32, (blocks, cols), 0) == at_block
        return jnp.dot(
            mask[...].astype(jnp.float32), pick.astype(jnp.float32),
            preferred_element_type=jnp.float32,
        )

    def filtered(source, j):
        for i in range(rows // BLOCK):
            block = pl.ds(i * BLOCK, BLOCK)
            out_ref[block, chunk(j)] = source[block, chunk(j)] * kept[pl.ds(i, 1), chunk(j)]

    y = at(r, c, other)
    load = pltpu.make_async_copy(d_ref, raw, local_sem.at[0])
    load.start()

    @pl.when(jnp.logical_not(is_hub))
    def _():
        sent.clear()
        hub = at(1 + r // 3, c, l)
        greet([hub, y])
        mask_dens(1)
        push(piece(own, 1), piece(own, 1), d_sem.at[own, 1], y)
        push(piece(own, 1), piece(own, 1), d_sem.at[own, 1], hub)
        for j in range(len(spans)):
            push(ham_from(other, j), held(r, l, j), h_sem.at[r, l, j], y)
            if j == 0:
                sent[0].wait_send()
        arrived(piece(yours, 1), d_sem.at[yours, 1])
        push(piece(yours, 1), piece(yours, 1), d_sem.at[yours, 1], hub)
        last = len(sent) - 1
        sent[1].wait_send()
        sent[last].wait_send()
        for j in range(len(spans)):
            push(ham_from(l, j), held(r, l, j), h_sem.at[r, l, j], hub)
            arrived(held(r, other, j), h_sem.at[r, other, j])
            push(held(r, other, j), held(r, other, j), h_sem.at[r, other, j], hub)
            if j > 0:
                sent[last + 2 * j - 1].wait_send()
                sent[last + 2 * j].wait_send()
        waited = {0, 1} | set(range(last, len(sent) - 2))
        kept[...] = widened(f_mask, l)
        for j in range(len(spans)):
            arrived(ends.at[:, chunk(j)], res_sem.at[j])
            filtered(ends, j)
        for i, copy in enumerate(sent):
            if i not in waited:
                copy.wait_send()

    @pl.when(is_hub)
    def _():
        sent.clear()
        end_row, far_row = 3 * r - 3, 3 - r
        far_end = 3 - end_row
        x, s = at(r, across, l), at(r, sibling, l)
        end, far = at(end_row, c, l), at(far_row, c, l)
        greet([y, x, s, end, far])

        def absorb(slot, half):
            def tile(i, _):
                at_rows = pl.ds(pl.multiple_of(half * rows + i * 128, 128), 128)
                high, low = split(dbuf[slot, at_rows, :])
                at_cols = pl.ds(pl.multiple_of(slot * width, width), width)
                dhi[at_rows, at_cols] = high
                dlo[at_rows, at_cols] = low
                return 0

            lax.fori_loop(0, rows // 128, tile, 0)

        def take(slot, half, *partners):
            arrived(piece(slot, half), d_sem.at[slot, half])
            for where in partners:
                push(piece(slot, half), piece(slot, half), d_sem.at[slot, half], where)
            absorb(slot, half)

        def straight(j):
            push(ham_from(l, j), held(r, l, j), h_sem.at[r, l, j], far)

        def relay(row, layer, j):
            arrived(held(row, layer, j), h_sem.at[row, layer, j])
            push(held(row, layer, j), held(row, layer, j), h_sem.at[row, layer, j], far)

        def relay_end(j):
            relay(end_row, l, j)
            relay(end_row, other, j)

        def split_ham(first, count, j):
            def part(i, _):
                i = first + i
                kept_blocks = masks[i // 2, i % 2, :, chunk(j)]
                for k in range(depth // BLOCK):
                    at_rows = pl.ds(pl.multiple_of(i * depth + k * BLOCK, BLOCK), BLOCK)
                    high, low = split(hbuf[at_rows, chunk(j)] * kept_blocks[k : k + 1, :])
                    hhi[at_rows, chunk(j)] = high
                    hlo[at_rows, chunk(j)] = low
                return 0

            lax.fori_loop(0, count, part, 0)

        def rows_of(half, target, first, count, j, add):
            at_depth = pl.ds(pl.multiple_of(first * depth, depth), count * depth)

            def tile(i, _):
                at_rows = pl.ds(pl.multiple_of(half * rows + i * 256, 256), 256)
                to_rows = pl.ds(pl.multiple_of(i * 256, 256), 256)
                high, h_high = dhi[at_rows, at_depth], hhi[at_depth, chunk(j)]
                total = jnp.dot(high, h_high, preferred_element_type=jnp.float32)
                total += jnp.dot(high, hlo[at_depth, chunk(j)], preferred_element_type=jnp.float32)
                total += jnp.dot(dlo[at_rows, at_depth], h_high, preferred_element_type=jnp.float32)
                if add:
                    total += target[to_rows, chunk(j)]
                target[to_rows, chunk(j)] = total
                return 0

            lax.fori_loop(0, rows // 256, tile, 0)

        near, near_count = (r - 1) * 2, 6
        late, late_count = far_end * 2, 2
        results = []

        def near_end(j):
            for layer in range(2):
                arrived(held(far_row, layer, j), h_sem.at[far_row, layer, j])
            split_ham(near, near_count, j)
            rows_of(1, ends, near, near_count, j, False)

        def late_end(j):
            for layer in range(2):
                arrived(held(far_end, layer, j), h_sem.at[far_end, layer, j])
            split_ham(late, late_count, j)
            rows_of(1, ends, late, late_count, j, True)
            copy = pltpu.make_async_remote_copy(
                src_ref=ends.at[:, chunk(j)], dst_ref=ends.at[:, chunk(j)],
                send_sem=res_send.at[j], recv_sem=res_sem.at[j],
                device_id=end, device_id_type=pl.DeviceIdType.MESH,
            )
            copy.start()
            results.append(copy)

        def near_own(j):
            rows_of(0, out_ref, near, near_count, j, False)

        def late_own(j):
            rows_of(0, out_ref, late, late_count, j, True)
            filtered(out_ref, j)

        def swap(j):
            push(ham_from(other, j), held(r, l, j), h_sem.at[r, l, j], y)

        straight(0)
        swap(0)
        straight(1)
        swap(1)
        mask_dens(0)
        for where in (x, s):
            push(piece(own, 0), piece(own, 0), d_sem.at[own, 0], where)
        straight(2)
        local_h = pltpu.make_async_copy(
            h_ref.at[:, pl.ds(pl.multiple_of(l * cols, cols), cols)],
            hbuf.at[ham_rows(r, l), :], local_sem.at[1],
        )
        local_h.start()
        wide, wide_other = widened(h_mask, l), widened(h_mask, other)
        kept[...] = widened(f_mask, l)
        for p in range(masks.shape[0]):
            blocks = slice(p * masks.shape[2], (p + 1) * masks.shape[2])
            masks[p, l] = wide[blocks]
            yours_mask[p] = wide_other[blocks]
        push(yours_mask, masks.at[:, l], mask_sem, y)
        absorb(own, 0)
        relay(r, other, 0)
        swap(2)
        relay(r, other, 1)
        swap(3)
        swap(4)
        take(own, 1, x, s)
        relay(r, other, 2)
        take(yours, 1, x, s)
        push(piece(own, 0), piece(own, 0), d_sem.at[own, 0], y)
        relay_end(0)
        take(across * 2 + l, 1, s)
        straight(3)
        relay_end(1)
        take(across * 2 + other, 1, s)
        relay(r, other, 3)
        away = (sibling + 2) % 4
        beside = [col * 2 + layer for col in (sibling, away) for layer in (l, other)]
        for slot in beside:
            take(slot, 1)
        local_h.wait()
        arrived(masks.at[:, other], mask_sem)
        near_end(0)
        take(yours, 0, x, s)
        late_end(0)
        take(across * 2 + l, 0, s)
        relay_end(2)
        take(across * 2 + other, 0, s)
        near_end(1)
        for slot in beside:
            take(slot, 0)
        relay_end(3)
        straight(4)
        relay(r, other, 4)
        late_end(1)
        relay_end(4)
        near_end(2)
        near_own(0)
        late_own(0)
        near_own(1)
        late_own(1)
        late_end(2)
        near_own(2)
        late_own(2)
        near_end(3)
        near_own(3)
        late_end(3)
        near_end(4)
        late_end(4)
        late_own(3)
        near_own(4)
        late_own(4)
        for copy in sent + results:
            copy.wait_send()


def chunk_spans(cols):
    quarter = cols // 4
    widths = [quarter] * 3 + [quarter // 2] * 2
    return [(sum(widths[:j]), width) for j, width in enumerate(widths)]


def product_of(dens, ham, packed, layers, grid_cols):
    rows, width = dens.shape
    depth, ham_cols = ham.shape
    cols = ham_cols // layers
    inner = layers * grid_cols * width
    planes = inner // (layers * depth)
    chunks = len(chunk_spans(cols))
    f32, bf16 = jnp.float32, jnp.bfloat16
    dma = pltpu.SemaphoreType.DMA
    return pl.pallas_call(
        kernel,
        out_shape=jax.ShapeDtypeStruct((rows, cols), f32),
        in_specs=[
            pl.BlockSpec(memory_space=pltpu.HBM),
            pl.BlockSpec(memory_space=pltpu.HBM),
            pl.BlockSpec(memory_space=pltpu.VMEM),
        ],
        out_specs=pl.BlockSpec(memory_space=pltpu.VMEM),
        scratch_shapes=[
            pltpu.VMEM((layers * grid_cols, 2 * rows, width), f32),
            pltpu.VMEM((inner, cols), f32),
            pltpu.VMEM((rows, width), f32),
            pltpu.VMEM((planes, layers, depth // BLOCK, cols), f32),
            pltpu.VMEM((planes, depth // BLOCK, cols), f32),
            pltpu.VMEM((rows // BLOCK, cols), f32),
            pltpu.VMEM((2 * rows, inner), bf16),
            pltpu.VMEM((2 * rows, inner), bf16),
            pltpu.VMEM((inner, cols), bf16),
            pltpu.VMEM((inner, cols), bf16),
            pltpu.VMEM((rows, cols), f32),
            dma((layers * grid_cols, 2)),
            dma((4, 2, chunks)),
            dma((chunks,)),
            dma((16 + 5 * chunks,)),
            dma((chunks,)),
            dma((2,)),
            dma,
        ],
        compiler_params=pltpu.CompilerParams(
            collective_id=0, has_side_effects=True, vmem_limit_bytes=50 * 2**20
        ),
    )(dens, ham, packed)


def lined_up(density, dens_mask, hamiltonian, ham_mask, filter_mask, *, layers, grid_cols):
    blocks, across = filter_mask.shape
    small = dens_mask[0].T
    small = jnp.pad(small, ((0, blocks - small.shape[0]), (0, across - small.shape[1])))
    packed = jnp.concatenate([filter_mask, small, ham_mask[0]], axis=0)
    return product_of(density[0], hamiltonian[0], packed, layers, grid_cols)


def gathered(density, dens_mask, hamiltonian, ham_mask, filter_mask):
    dens = lax.all_gather(density * expand(dens_mask), "col", axis=2, tiled=True)[0]
    ham = lax.all_gather(masked_ham(hamiltonian, ham_mask), "row", axis=0, tiled=True)
    part = jnp.dot(dens, ham, precision=lax.Precision.HIGHEST, preferred_element_type=jnp.float32)
    return lax.psum_scatter(part * expand(filter_mask), "layer", scatter_dimension=1, tiled=True)


def solution(mesh):
    sizes = dict(mesh.shape)
    layers, grid_cols = sizes["layer"], sizes["col"]
    body = gathered
    if sizes == {"row": 4, "col": 4, "layer": 2}:
        body = functools.partial(lined_up, layers=layers, grid_cols=grid_cols)
    return jax.shard_map(
        body,
        mesh=mesh,
        in_specs=(
            P("layer", "row", "col"),
            P("layer", "row", "col"),
            P("layer", "row", "col"),
            P("layer", None, "col"),
            P("row", "col"),
        ),
        out_specs=P("row", ("col", "layer")),
        check_vma=False,
    )
```
